32 devices in a mesh: gx: 16 (over z, x, core), gy: 2 (over y).
Axes of the slice: x: 2, y: 2, z: 4, core: 2. Of those that a mesh axis runs over, the one named last changes fastest.
Arguments:
- field: bfloat16 [512, 128, 512], P('gx', 'gy'), may hold values from -6 to 6
- perm_class: int32 [512, 4096], P('gx', 'gy'), may hold values from 0 to 7
- perm_table: float32 [8], replicated, may hold values from 0.05 to 0.5
- forcing: float32 [512, 4096], P('gx', 'gy'), may hold values from -6 to 6
- spec_weight: bfloat16 [2, 16, 16, 16, 16], replicated, may hold values from -1 to 1
- mix_weight: bfloat16 [16, 16], replicated, may hold values from -1.5 to 1.5
- proj: float32 [16], replicated, may hold values from -1.5 to 1.5
Outputs:
- residual: float32 [512, 4096], P('gx', 'gy')
- grad_field: bfloat16 [512, 128, 512], P('gx', 'gy')
- spec_grad: float32 [2, 16, 16, 16, 16], replicated
The draws below stay inside these ranges and needn't reach their ends.
All inputs are finite; a program needn't handle non-finite values.
Results may differ from the reference program's by a relative error of at most 0.015.
Values may be sent and summed in bfloat16 or wider, within the bound.
A program may use at most 128 MiB of HBM per device.

```python
import math
import jax
import jax.numpy as jnp
from jax import lax

C = 16
KX = 16
KY = 16
CLASSES = 8
NZ = 32
NX = 512
NY = 128


def with_ends(result, rng, least, largest):
    index_at = [jax.random.randint(jax.random.fold_in(rng, axis), (), 0, length) for axis, length in enumerate(result.shape)]
    longest = result.shape.index(max(result.shape))
    neighbour = index_at[:longest] + [(index_at[longest] + 1) % result.shape[longest]] + index_at[longest + 1:]
    return result.at[tuple(index_at)].set(least).at[tuple(neighbour)].set(largest)


def levels(stream_key, shape, pieces, least, high):
    level, own = 1.0, jax.random.fold_in(stream_key, 6)
    for dim, parts in pieces:
        heights = jnp.exp(jax.random.uniform(jax.random.fold_in(own, dim), (parts,), jnp.float32, least / len(pieces), high / len(pieces)))
        level = level * jnp.repeat(heights, shape[dim] // parts).reshape([-1 if axis == dim else 1 for axis in range(len(shape))])
    return level


def normal_values(rng, dims, spread, most, cuts=(), held_as=jnp.bfloat16):
    drawn = spread * jax.random.normal(rng, dims, jnp.float32)
    if cuts:
        drawn = drawn * levels(rng, dims, cuts, -0.22, 0.18)
    return jnp.clip(drawn, -most, most).astype(held_as)


def setup_inputs(seed: int = 0) -> dict:
    arg_keys = jax.random.split(jax.random.key(seed), 8)
    field = normal_values(arg_keys[0], (NX, NY, NZ * C), 1.0, 6.0, ((0, 16), (1, 2)))
    perm_class = with_ends(jax.random.randint(arg_keys[1], (NX, NY * NZ), 0, CLASSES), jax.random.fold_in(arg_keys[1], 1), 0, CLASSES - 1).astype(jnp.int32)
    perm_table = jnp.clip(jnp.exp(jax.random.uniform(arg_keys[2], (CLASSES,), jnp.float32, math.log(0.05), math.log(0.5))), 0.05, 0.5)
    forcing = normal_values(arg_keys[3], (NX, NY * NZ), 1.0, 6.0, ((0, 16), (1, 2)), jnp.float32)
    spec_weight = normal_values(arg_keys[4], (2, KX, KY, C, C), (2 * C) ** -0.5, 1.0)
    mix_weight = normal_values(arg_keys[5], (C, C), C ** -0.5, 1.5)
    proj = normal_values(arg_keys[6], (C,), C ** -0.5, 1.5, (), jnp.float32)
    return dict(field=field, perm_class=perm_class, perm_table=perm_table, forcing=forcing, spec_weight=spec_weight, mix_weight=mix_weight, proj=proj)


HIGHEST = lax.Precision.HIGHEST
ROOT_HALF = 0.7071067811865476
INV_ROOT_TWO_PI = 0.3989422804014327

def contract(form, left, right):
    return jnp.einsum(form, left, right, precision=HIGHEST)

def angle_tables(positions, length, count, scale):
    frequencies = jnp.arange(count, dtype=jnp.int32) - count // 2
    turns = positions[:, None] * frequencies[None, :] % length
    angle = turns.astype(jnp.float32) * (2.0 * math.pi / length)
    return (jnp.cos(angle) * scale, jnp.sin(angle) * scale)

def x_table(positions, length, scale):
    cosine, sine = angle_tables(positions, length, KX, scale)
    return jnp.concatenate([cosine, -sine], axis=1).astype(jnp.bfloat16)

def y_tables(length):
    positions = jnp.arange(length, dtype=jnp.int32)
    forward_cos, forward_sin = angle_tables(positions, length, KY, 1.0 / math.sqrt(length))
    inverse_cos, inverse_sin = angle_tables(positions, length, KY, 1.0 / math.sqrt(KY))
    return (forward_cos, forward_sin, inverse_cos, inverse_sin)

def y_forward(part, forward_cos, forward_sin):
    real_part = part[..., 0, :, :, :]
    imaginary = part[..., 1, :, :, :]
    form = '...ayc,yb->...abc'
    real_result = contract(form, real_part, forward_cos) + contract(form, imaginary, forward_sin)
    imag_result = contract(form, imaginary, forward_cos) - contract(form, real_part, forward_sin)
    return jnp.stack([real_result, imag_result], axis=-4)

def mix_modes(coefficients, weight_real, weight_imaginary):
    real_part = coefficients[..., 0, :, :, :]
    imaginary = coefficients[..., 1, :, :, :]
    form = '...abc,abco->...abo'
    real_result = contract(form, real_part, weight_real) - contract(form, imaginary, weight_imaginary)
    imag_result = contract(form, real_part, weight_imaginary) + contract(form, imaginary, weight_real)
    return jnp.stack([real_result, imag_result], axis=-4)

def y_inverse(mixed, inverse_cos, inverse_sin):
    real_part = mixed[..., 0, :, :, :]
    imaginary = mixed[..., 1, :, :, :]
    form = '...abc,yb->...ayc'
    real_result = contract(form, real_part, inverse_cos) - contract(form, imaginary, inverse_sin)
    imag_result = contract(form, real_part, inverse_sin) + contract(form, imaginary, inverse_cos)
    return jnp.stack([real_result, imag_result], axis=-4)

def y_inverse_adjoint(grad_back, inverse_cos, inverse_sin):
    real_part = grad_back[..., 0, :, :, :]
    imaginary = grad_back[..., 1, :, :, :]
    form = '...ayc,yb->...abc'
    real_result = contract(form, real_part, inverse_cos) + contract(form, imaginary, inverse_sin)
    imag_result = contract(form, imaginary, inverse_cos) - contract(form, real_part, inverse_sin)
    return jnp.stack([real_result, imag_result], axis=-4)

def mix_adjoint(coefficients, grad_out, weight_real, weight_imaginary):
    coef_real = coefficients[..., 0, :, :, :]
    coef_imaginary = coefficients[..., 1, :, :, :]
    grad_real = grad_out[..., 0, :, :, :]
    grad_imaginary = grad_out[..., 1, :, :, :]
    form = '...abo,abco->...abc'
    input_real = contract(form, grad_real, weight_real) + contract(form, grad_imaginary, weight_imaginary)
    input_imaginary = contract(form, grad_imaginary, weight_real) - contract(form, grad_real, weight_imaginary)
    outer = '...abc,...abo->abco'
    weight_grad_real = contract(outer, coef_real, grad_real) + contract(outer, coef_imaginary, grad_imaginary)
    weight_grad_imaginary = contract(outer, coef_real, grad_imaginary) - contract(outer, coef_imaginary, grad_real)
    return (jnp.stack([input_real, input_imaginary], axis=-4), jnp.stack([weight_grad_real, weight_grad_imaginary], axis=0))

def y_forward_adjoint(grad_coef, forward_cos, forward_sin):
    real_part = grad_coef[..., 0, :, :, :]
    imaginary = grad_coef[..., 1, :, :, :]
    form = '...abc,yb->...ayc'
    real_result = contract(form, real_part, forward_cos) - contract(form, imaginary, forward_sin)
    imag_result = contract(form, real_part, forward_sin) + contract(form, imaginary, forward_cos)
    return jnp.stack([real_result, imag_result], axis=-4)

def gelu_value(preact):
    return 0.5 * preact * (1.0 + lax.erf(preact * ROOT_HALF))

def gelu_slope(preact):
    return 0.5 * (1.0 + lax.erf(preact * ROOT_HALF)) + preact * jnp.exp(-0.5 * preact * preact) * INV_ROOT_TWO_PI

def apply_operator(values, permeability):
    centre_value = values[1:-1, 1:-1, 1:-1]
    centre_perm = permeability[1:-1, 1:-1, 1:-1]
    total = jnp.zeros_like(centre_value)
    for axis in range(3):
        for offset in (0, 2):
            index = [slice(1, -1), slice(1, -1), slice(1, -1)]
            index[axis] = slice(offset, offset + centre_value.shape[axis])
            neighbour_value = values[tuple(index)]
            neighbour_perm = permeability[tuple(index)]
            total = total + 0.5 * (centre_perm + neighbour_perm) * (centre_value - neighbour_value)
    return total

def reference(field, perm_class, perm_table, forcing, spec_weight, mix_weight, proj):
    positions = jnp.arange(NX, dtype=jnp.int32)
    forward_table = x_table(positions, NX, 1.0 / math.sqrt(NX))
    inverse_table = x_table(positions, NX, 1.0 / math.sqrt(KX))
    forward_cos, forward_sin, inverse_cos, inverse_sin = y_tables(NY)
    weight_real = spec_weight[0].astype(jnp.float32)
    weight_imaginary = spec_weight[1].astype(jnp.float32)
    volume = field.reshape(NX, NY, NZ, C)

    def forward_plane(plane_index):
        plane = lax.dynamic_index_in_dim(volume, plane_index, 2, keepdims=False)
        flat = plane.reshape(NX, NY * C)
        part = jnp.dot(forward_table.T, flat, preferred_element_type=jnp.float32).reshape(2, KX, NY, C)
        coefficients = y_forward(part, forward_cos, forward_sin)
        mixed = mix_modes(coefficients, weight_real, weight_imaginary)
        back = y_inverse(mixed, inverse_cos, inverse_sin).reshape(2 * KX, NY * C).astype(jnp.bfloat16)
        spectral = jnp.dot(inverse_table, back, preferred_element_type=jnp.float32).astype(jnp.bfloat16)
        local = jnp.dot(plane.reshape(NX * NY, C), mix_weight, preferred_element_type=jnp.float32)
        preact = spectral.reshape(NX * NY, C).astype(jnp.float32) + local
        pressure = lax.optimization_barrier(jnp.sum(gelu_value(preact) * proj, axis=1)).reshape(NX, NY)
        return (spectral, coefficients, pressure)
    spectral_all, coef_all, pressure_all = lax.map(forward_plane, jnp.arange(NZ, dtype=jnp.int32))
    pressure = jnp.transpose(pressure_all, (1, 2, 0))
    permeability = perm_table[perm_class].reshape(NX, NY, NZ)
    padded_perm = jnp.pad(permeability, 1)
    applied = apply_operator(jnp.pad(pressure, 1), padded_perm)
    residual = applied - forcing.reshape(NX, NY, NZ)
    grad_pressure = apply_operator(jnp.pad(residual, 1), padded_perm)

    def backward_plane(carry, plane_index):
        plane = lax.dynamic_index_in_dim(volume, plane_index, 2, keepdims=False)
        spectral = lax.dynamic_index_in_dim(spectral_all, plane_index, 0, keepdims=False)
        coefficients = lax.dynamic_index_in_dim(coef_all, plane_index, 0, keepdims=False)
        slope_source = lax.dynamic_index_in_dim(grad_pressure, plane_index, 2, keepdims=False).reshape(NX * NY, 1)
        local = jnp.dot(plane.reshape(NX * NY, C), mix_weight, preferred_element_type=jnp.float32)
        preact = spectral.reshape(NX * NY, C).astype(jnp.float32) + local
        grad_pre = (proj * slope_source * gelu_slope(preact)).astype(jnp.bfloat16)
        grad_back = jnp.dot(inverse_table.T, grad_pre.reshape(NX, NY * C), preferred_element_type=jnp.float32)
        grad_out = y_inverse_adjoint(grad_back.reshape(2, KX, NY, C), inverse_cos, inverse_sin)
        grad_coef, grad_weight = mix_adjoint(coefficients, grad_out, weight_real, weight_imaginary)
        grad_part = y_forward_adjoint(grad_coef, forward_cos, forward_sin).reshape(2 * KX, NY * C).astype(jnp.bfloat16)
        grad_spec = jnp.dot(forward_table, grad_part, preferred_element_type=jnp.float32).astype(jnp.bfloat16)
        grad_local = jnp.dot(grad_pre, mix_weight.T, preferred_element_type=jnp.float32)
        grad_plane = (grad_spec.reshape(NX * NY, C).astype(jnp.float32) + grad_local).astype(jnp.bfloat16)
        return (carry + grad_weight, grad_plane.reshape(NX, NY, C))
    spec_grad, grad_planes = lax.scan(backward_plane, jnp.zeros((2, KX, KY, C, C), jnp.float32), jnp.arange(NZ, dtype=jnp.int32))
    grad_field = jnp.transpose(grad_planes, (1, 2, 0, 3)).reshape(NX, NY, NZ * C)
    return (residual.reshape(NX, NY * NZ), grad_field, spec_grad)
```

```python
import functools
import math

import jax
import jax.numpy as jnp
import numpy as np
from jax import lax
from jax.experimental import pallas as pl
from jax.experimental.pallas import tpu as pltpu
from jax.sharding import PartitionSpec as P

C = 16
KX = 16
KY = 16
CLASSES = 8
LANES = 128
ROOT_HALF = 0.7071067811865476
INV_ROOT_TWO_PI = 0.3989422804014327
MESH = pl.DeviceIdType.MESH
F32 = jnp.float32
BF16 = jnp.bfloat16


def dot(left, right):
    return jnp.dot(left, right, preferred_element_type=F32)


def dot_first(left, right):
    return lax.dot_general(left, right, (((0,), (0,)), ((), ())), preferred_element_type=F32)


def split_dot(value, right):
    high = value.astype(BF16)
    low = (value - high.astype(F32)).astype(BF16)
    return dot(high, right) + dot(low, right)


def lane_iota(shape):
    return lax.broadcasted_iota(jnp.int32, shape, len(shape) - 1)


def group_roll(value, amount):
    if amount == 0:
        return value
    inside = lane_iota(value.shape) % C >= amount
    return jnp.where(
        inside, pltpu.roll(value, amount, 1), pltpu.roll(value, LANES - C + amount, 1)
    )


def kernel(
    gxn,
    gyn,
    owners,
    rows_x,
    rows_y,
    depth,
    field_ref,
    class_ref,
    table_ref,
    forcing_ref,
    x_ref,
    y_ref,
    weight_ref,
    mix_ref,
    mix_t_ref,
    proj_ref,
    sum_ref,
    spread_ref,
    residual_ref,
    grad_ref,
    spec_ref,
    fwd_ref,
    inv_ref,
    send_ref,
    recv_ref,
    out_ref,
    gout_ref,
    slope_ref,
    pre_ref,
    press_ref,
    coef_ref,
    x_send,
    x_recv,
    y_send,
    y_recv,
    send_sem,
    recv_sem,
    halo_send,
    halo_recv,
):
    n = gxn * gyn
    gx = lax.axis_index("gx")
    gy = lax.axis_index("gy")
    me = gx * gyn + gy
    apart = n // owners
    own = me // apart
    owner = me % apart == 0
    cells = rows_x * rows_y
    width = depth * C
    block = 2 * KX * KY // owners
    half = block // 2
    per = LANES // depth
    span = rows_y * depth
    columns = owners * block

    def if_owner(body):
        if apart == 1:
            body()
        else:
            pl.when(owner)(body)

    def place(index):
        return (index // gyn, index % gyn)

    barrier = pltpu.get_barrier_semaphore()

    def greet(k, carry):
        target = lax.rem(me + k, n)
        pl.semaphore_signal(barrier, inc=1, device_id=place(target), device_id_type=MESH)
        return carry

    lax.fori_loop(1, n, greet, 0)

    def fill(which, ref):
        def body(x, carry):
            first = x_ref[2 * which, pl.ds(x, 1), :]
            second = x_ref[2 * which + 1, pl.ds(x, 1), :]
            made = first * y_ref[2 * which] + second * y_ref[2 * which + 1]
            start = pl.multiple_of(x * rows_y, rows_y)
            ref[pl.ds(start, rows_y), :] = made.astype(BF16)
            return carry

        lax.fori_loop(0, rows_x, body, 0)

    fill(0, fwd_ref)
    pl.semaphore_wait(barrier, n - 1)

    classes = class_ref[...]
    perm = jnp.zeros(classes.shape, F32)
    for level in range(CLASSES):
        perm = jnp.where(classes == level, table_ref[level], perm)

    sides = (
        (gx > 0, (gx - 1, gy), x_send, x_recv, 0),
        (gx < gxn - 1, (gx + 1, gy), x_send, x_recv, 1),
        (gy > 0, (gx, gy - 1), y_send, y_recv, 0),
        (gy < gyn - 1, (gx, gy + 1), y_send, y_recv, 1),
    )

    def halo_copy(turn, side):
        _, target, source, landing, end = sides[side]
        return pltpu.make_async_remote_copy(
            src_ref=source.at[turn, end],
            dst_ref=landing.at[turn, 1 - end],
            send_sem=halo_send.at[turn, side],
            recv_sem=halo_recv.at[turn, side ^ 1],
            device_id=target,
            device_id_type=MESH,
        )

    def halo_start(turn, value):
        x_send[turn, 0] = value[0:1, :]
        x_send[turn, 1] = value[rows_x - 1 : rows_x, :]
        y_send[turn, 0] = value[:, 0:LANES]
        y_send[turn, 1] = value[:, span - LANES : span]
        for side in range(4):
            there, _, _, landing, end = sides[side]

            @pl.when(there)
            def _():
                halo_copy(turn, side).start()

            @pl.when(jnp.logical_not(there))
            def _():
                landing[turn, end] = jnp.zeros(landing.shape[2:], F32)

    def halo_wait(turn):
        for side in range(4):
            there, _, _, landing, end = sides[side]

            @pl.when(there)
            def _():
                copy = halo_copy(turn, side)
                copy.wait_send()
                pltpu.make_async_copy(
                    landing.at[turn, end], landing.at[turn, end], halo_recv.at[turn, side]
                ).wait()

    row = lax.broadcasted_iota(jnp.int32, (rows_x, span), 0)
    layer = lane_iota((rows_x, span)) % depth
    lane = lane_iota((rows_x, LANES))

    def neighbours(turn, value):
        below = jnp.where(row == 0, x_recv[turn, 0], pltpu.roll(value, 1, 0))
        above = jnp.where(row == rows_x - 1, x_recv[turn, 1], pltpu.roll(value, rows_x - 1, 0))
        moved = pltpu.roll(value, depth, 1)
        edge = jnp.where(lane < depth, pltpu.roll(y_recv[turn, 0], depth, 1), moved[:, :LANES])
        left = jnp.concatenate([edge, moved[:, LANES:]], axis=1)
        moved = pltpu.roll(value, span - depth, 1)
        edge = jnp.where(
            lane >= LANES - depth,
            pltpu.roll(y_recv[turn, 1], LANES - depth, 1),
            moved[:, span - LANES :],
        )
        right = jnp.concatenate([moved[:, : span - LANES], edge], axis=1)
        under = jnp.where(layer == 0, 0.0, pltpu.roll(value, 1, 1))
        over = jnp.where(layer == depth - 1, 0.0, pltpu.roll(value, span - 1, 1))
        return (below, above, left, right, under, over)

    halo_start(0, perm)

    def all_to_all(phase, right_ref, table):
        group = LANES // block

        def body(part, carry):
            start = pl.multiple_of(part * LANES, LANES)
            made = dot_first(table[:, pl.ds(start, LANES)], right_ref[...])
            first = part * group
            send_ref[pl.ds(first, group)] = made.astype(BF16).reshape(group, block, width)

            def push(k, inner):
                target = (first + k) * apart

                @pl.when(target != me)
                def _():
                    pltpu.make_async_remote_copy(
                        src_ref=send_ref.at[first + k],
                        dst_ref=recv_ref.at[phase, me],
                        send_sem=send_sem.at[2 * phase],
                        recv_sem=recv_sem.at[2 * phase],
                        device_id=place(target),
                        device_id_type=MESH,
                    ).start()

                return inner

            lax.fori_loop(0, group, push, 0)
            return carry

        lax.fori_loop(0, columns // LANES, body, 0)

    def wait_chunks(ref, count, sem):
        held = ref.shape[0]
        for _ in range(count // held):
            pltpu.make_async_copy(ref, ref, sem).wait()
        if count % held:
            rest = ref.at[pl.ds(0, count % held)]
            pltpu.make_async_copy(rest, rest, sem).wait()

    def wait_owned(ref, sem):
        if_owner(lambda: wait_chunks(ref, owners - 1, sem))
        if apart > 1:
            pl.when(jnp.logical_not(owner))(lambda: wait_chunks(ref, owners, sem))

    def all_to_all_sum(phase):
        recv_ref[phase, me] = send_ref[own]
        wait_chunks(recv_ref.at[phase], n - 1, recv_sem.at[2 * phase])

        def body(k, total):
            return total + recv_ref[phase, k].astype(F32)

        total = lax.fori_loop(0, n, body, jnp.zeros((block, width), F32))

        def lines(part):
            return jnp.concatenate(
                [part[:, k : k + LANES] for k in range(0, width, LANES)], axis=0
            )

        return lines(total[:half]), lines(total[half:])

    parts = width // LANES

    def unlines(part):
        return jnp.concatenate([part[k * half : (k + 1) * half] for k in range(parts)], axis=1)

    def weights(shift):
        real = jnp.concatenate([weight_ref[0, shift]] * parts, axis=0)
        imaginary = jnp.concatenate([weight_ref[1, shift]] * parts, axis=0)
        return real, imaginary

    def all_gather(phase, ref):
        def push(k, carry):
            target = lax.rem(me + k, n)
            pltpu.make_async_remote_copy(
                src_ref=ref.at[own],
                dst_ref=ref.at[own],
                send_sem=send_sem.at[2 * phase + 1],
                recv_sem=recv_sem.at[2 * phase + 1],
                device_id=place(target),
                device_id_type=MESH,
            ).start()
            return carry

        lax.fori_loop(1, n, push, 0)

    def all_gather_wait(phase, ref):
        wait_owned(ref, recv_sem.at[2 * phase + 1])
        if_owner(lambda: wait_chunks(ref, n - 1, send_sem.at[2 * phase + 1]))
        wait_owned(send_ref, send_sem.at[2 * phase])

    all_to_all(0, field_ref, fwd_ref)
    fill(1, inv_ref)

    @if_owner
    def _():
        real, imaginary = all_to_all_sum(0)
        coef_ref[0] = real
        coef_ref[1] = imaginary
        out_real = jnp.zeros_like(real)
        out_imag = jnp.zeros_like(real)
        for shift in range(C):
            w_real, w_imag = weights(shift)
            c_real = group_roll(real, shift)
            c_imag = group_roll(imaginary, shift)
            out_real = out_real + (c_real * w_real - c_imag * w_imag)
            out_imag = out_imag + (c_real * w_imag + c_imag * w_real)
        mixed = jnp.concatenate([unlines(out_real), unlines(out_imag)], axis=0)
        out_ref[own] = mixed.astype(BF16)
        all_gather(0, out_ref)

    all_gather_wait(0, out_ref)

    chunk = 4 * rows_y
    step = mix_ref.shape[0]

    def local(value, matrix):
        return jnp.concatenate(
            [dot(value[:, k : k + step], matrix) for k in range(0, width, step)], axis=1
        )

    def activate(index, carry):
        here = pl.ds(pl.multiple_of(index * chunk, chunk), chunk)
        spectral = dot(inv_ref[here, :], out_ref[...].reshape(columns, width))
        preact = spectral.astype(BF16).astype(F32) + local(field_ref[here, :], mix_ref[...])
        bell = 0.5 * (1.0 + lax.erf(preact * ROOT_HALF))
        tail = preact * jnp.exp(-0.5 * preact * preact) * INV_ROOT_TWO_PI
        slope_ref[here, :] = (bell + tail) * proj_ref[...]
        press_ref[here, :] = split_dot(preact * bell * proj_ref[...], sum_ref[...])
        return carry

    lax.fori_loop(0, cells // chunk, activate, 0)

    def gathered(index):
        made = press_ref[pl.ds(index * per, rows_x, stride=rows_y), :]
        for k in range(1, per):
            other = press_ref[pl.ds(index * per + k, rows_x, stride=rows_y), :]
            made = jnp.where(lane // depth == k, other, made)
        return made

    pressure = jnp.concatenate([gathered(k) for k in range(rows_y // per)], axis=1)
    halo_start(1, pressure)
    halo_wait(0)
    means = [0.5 * (perm + other) for other in neighbours(0, perm)]
    halo_wait(1)

    def operator(turn, value):
        total = jnp.zeros_like(value)
        for mean, other in zip(means, neighbours(turn, value)):
            total = total + mean * (value - other)
        return total

    residual = operator(1, pressure) - forcing_ref[...]
    residual_ref[...] = residual
    halo_start(2, residual)
    halo_wait(2)
    slope_source = operator(2, residual)
    for k in range(rows_y // per):
        piece = slope_source[:, k * LANES : (k + 1) * LANES]
        for j in range(per):
            press_ref[pl.ds(k * per + j, rows_x, stride=rows_y), :] = jnp.where(
                lane // depth == j, piece, 0.0
            )

    def differentiate(index, carry):
        here = pl.ds(pl.multiple_of(index * chunk, chunk), chunk)
        wide = split_dot(press_ref[here, :], spread_ref[...])
        pre_ref[here, :] = (wide * slope_ref[here, :]).astype(BF16)
        return carry

    lax.fori_loop(0, cells // chunk, differentiate, 0)

    all_to_all(1, pre_ref, inv_ref)

    @if_owner
    def _():
        g_real, g_imag = all_to_all_sum(1)
        real = coef_ref[0]
        imaginary = coef_ref[1]
        in_real = jnp.zeros_like(real)
        in_imag = jnp.zeros_like(real)
        grads = [[jnp.zeros((half, LANES), F32) for _ in range(C * C // LANES)] for _ in range(2)]
        spot = lane_iota((half, LANES))
        for shift in range(C):
            w_real, w_imag = weights(shift)
            in_real = in_real + group_roll(g_real * w_real + g_imag * w_imag, (C - shift) % C)
            in_imag = in_imag + group_roll(g_imag * w_real - g_real * w_imag, (C - shift) % C)
            c_real = group_roll(real, shift)
            c_imag = group_roll(imaginary, shift)
            both = (c_real * g_real + c_imag * g_imag, c_real * g_imag - c_imag * g_real)
            for which in range(2):
                total = both[which][:half]
                for k in range(1, parts):
                    total = total + both[which][k * half : (k + 1) * half]
                turn = C
                while turn < LANES:
                    total = total + pltpu.roll(total, turn, 1)
                    turn *= 2
                for k in range(C * C // LANES):
                    source = k * (LANES // C) + spot // C
                    match = (spot % C - source + C) % C == shift
                    grads[which][k] = jnp.where(match, total, grads[which][k])
        message = jnp.concatenate(
            [
                jnp.concatenate([unlines(in_real)] + grads[0], axis=1),
                jnp.concatenate([unlines(in_imag)] + grads[1], axis=1),
            ],
            axis=0,
        )
        gout_ref[own] = message.astype(BF16)
        all_gather(1, gout_ref)

    all_gather_wait(1, gout_ref)

    def finish(index, carry):
        here = pl.ds(pl.multiple_of(index * chunk, chunk), chunk)
        spectral = dot(fwd_ref[here, :], gout_ref[:, :, :width].reshape(columns, width))
        total = spectral.astype(BF16).astype(F32) + local(pre_ref[here, :], mix_t_ref[...])
        grad_ref[here, :] = total.astype(BF16)
        return carry

    lax.fori_loop(0, cells // chunk, finish, 0)

    def report(k, carry):
        terms = gout_ref[k, :, width:].astype(F32)
        spec_ref[0, k] = terms[:half]
        spec_ref[1, k] = terms[half:]
        return carry

    lax.fori_loop(0, owners, report, 0)


def angle_tables(positions, frequencies, length, scale):
    turns = positions[:, None] * frequencies[None, :] % length
    angle = turns.astype(F32) * (2.0 * math.pi / length)
    return (jnp.cos(angle) * scale, jnp.sin(angle) * scale)


def shards(field, perm_class, perm_table, forcing, spec_weight, mix_weight, proj):
    gxn = lax.axis_size("gx")
    gyn = lax.axis_size("gy")
    n = gxn * gyn
    gx = lax.axis_index("gx")
    gy = lax.axis_index("gy")
    me = gx * gyn + gy
    rows_x, rows_y, width = field.shape
    depth = width // C
    cells = rows_x * rows_y
    span_x = rows_x * gxn
    span_y = rows_y * gyn
    owners = min(n, KX * KY // 8)
    modes = KX * KY // owners
    block = 2 * modes
    columns = owners * block

    column = np.arange(columns)
    mode = column // block * modes + column % modes
    imag = jnp.asarray(column % block >= modes)
    f_x = jnp.asarray(mode // KY - KX // 2, jnp.int32)
    f_y = jnp.asarray(mode % KY - KY // 2, jnp.int32)
    at_x = gx * rows_x + jnp.arange(rows_x, dtype=jnp.int32)
    at_y = gy * rows_y + jnp.arange(rows_y, dtype=jnp.int32)
    x_rows, y_rows = [], []
    for x_scale, y_scale in (
        (1.0 / math.sqrt(span_x), 1.0 / math.sqrt(span_y)),
        (1.0 / math.sqrt(KX), 1.0 / math.sqrt(KY)),
    ):
        cosine, sine = angle_tables(at_x, f_x, span_x, x_scale)
        x_cos = cosine.astype(BF16).astype(F32)
        x_sin = (-sine).astype(BF16).astype(F32)
        y_cos, y_sin = angle_tables(at_y, f_y, span_y, y_scale)
        x_rows += [jnp.where(imag, x_sin, x_cos), jnp.where(imag, -x_cos, x_sin)]
        y_rows += [y_cos, y_sin]
    x_rows = jnp.stack(x_rows)
    y_rows = jnp.stack(y_rows)

    own = lax.dynamic_slice_in_dim(spec_weight.reshape(2, KX * KY, C, C), me // (n // owners) * modes, modes, 1)
    own = jnp.tile(own.astype(F32), (1, 1, 1, LANES // C))
    shift = np.arange(C)[:, None, None]
    source = np.arange(C)[None, :, None]
    output = np.arange(LANES)[None, None, :] % C
    chosen = jnp.asarray((output - shift) % C == source)
    skewed = jnp.sum(jnp.where(chosen[None, :, None], own[:, None], 0.0), axis=3)

    step = min(256, width)
    copies = step // C
    eye = jnp.asarray(np.kron(np.eye(copies), np.ones((C, C))), BF16)
    mix = jnp.tile(mix_weight, (copies, copies)) * eye
    mix_t = jnp.tile(mix_weight.T, (copies, copies)) * eye
    proj_row = jnp.tile(proj, depth).reshape(1, width)
    gather = np.arange(width)[:, None] // C == np.arange(LANES)[None, :] % depth
    total = jnp.asarray(gather, BF16)
    spread = jnp.asarray(gather.T, BF16)

    vmem = pl.BlockSpec(memory_space=pltpu.VMEM)
    smem = pl.BlockSpec(memory_space=pltpu.SMEM)
    residual, grad_field, spec = pl.pallas_call(
        functools.partial(kernel, gxn, gyn, owners, rows_x, rows_y, depth),
        out_shape=(
            jax.ShapeDtypeStruct((rows_x, rows_y * depth), F32),
            jax.ShapeDtypeStruct((cells, width), BF16),
            jax.ShapeDtypeStruct((2, owners, modes, C * C), F32),
        ),
        in_specs=[vmem, vmem, smem] + [vmem] * 9,
        out_specs=(vmem, vmem, vmem),
        scratch_shapes=[
            pltpu.VMEM((cells, columns), BF16),
            pltpu.VMEM((cells, columns), BF16),
            pltpu.VMEM((owners, block, width), BF16),
            pltpu.VMEM((2, n, block, width), BF16),
            pltpu.VMEM((owners, block, width), BF16),
            pltpu.VMEM((owners, block, width + C * C), BF16),
            pltpu.VMEM((cells, width), F32),
            pltpu.VMEM((cells, width), BF16),
            pltpu.VMEM((cells, LANES), F32),
            pltpu.VMEM((2, modes * width // LANES, LANES), F32),
            pltpu.VMEM((3, 2, 1, rows_y * depth), F32),
            pltpu.VMEM((3, 2, 1, rows_y * depth), F32),
            pltpu.VMEM((3, 2, rows_x, LANES), F32),
            pltpu.VMEM((3, 2, rows_x, LANES), F32),
            pltpu.SemaphoreType.DMA((4,)),
            pltpu.SemaphoreType.DMA((4,)),
            pltpu.SemaphoreType.DMA((3, 4)),
            pltpu.SemaphoreType.DMA((3, 4)),
        ],
        compiler_params=pltpu.CompilerParams(
            collective_id=0, has_side_effects=True, vmem_limit_bytes=60 * 1024 * 1024
        ),
        name="fourier_darcy",
    )(
        field.reshape(cells, width),
        perm_class,
        perm_table,
        forcing,
        x_rows,
        y_rows,
        skewed,
        mix,
        mix_t,
        proj_row,
        total,
        spread,
    )
    spec_grad = spec.reshape(2, KX, KY, C, C)
    return (residual, grad_field.reshape(rows_x, rows_y, width), spec_grad)


def solution(mesh):
    placed = (P("gx", "gy", None), P("gx", "gy"), P(), P("gx", "gy"), P(), P(), P())
    return jax.shard_map(
        shards,
        mesh=mesh,
        in_specs=placed,
        out_specs=(P("gx", "gy"), P("gx", "gy", None), P()),
        check_vma=False,
    )
```

```python
import functools
import math

import jax
import jax.numpy as jnp
import numpy as np
from jax import lax
from jax.experimental import pallas as pl
from jax.experimental.pallas import tpu as pltpu
from jax.sharding import PartitionSpec as P

C = 16
KX = 16
KY = 16
CLASSES = 8
LANES = 128
ROOT_HALF = 0.7071067811865476
INV_ROOT_TWO_PI = 0.3989422804014327
MESH = pl.DeviceIdType.MESH
F32 = jnp.float32
BF16 = jnp.bfloat16


def dot(left, right):
    return jnp.dot(left, right, preferred_element_type=F32)


def dot_first(left, right):
    return lax.dot_general(left, right, (((0,), (0,)), ((), ())), preferred_element_type=F32)


def split_dot(value, right):
    high = value.astype(BF16)
    low = (value - high.astype(F32)).astype(BF16)
    return dot(high, right) + dot(low, right)


def lane_iota(shape):
    return lax.broadcasted_iota(jnp.int32, shape, len(shape) - 1)


def group_roll(value, amount):
    if amount == 0:
        return value
    inside = lane_iota(value.shape) % C >= amount
    return jnp.where(
        inside, pltpu.roll(value, amount, 1), pltpu.roll(value, LANES - C + amount, 1)
    )


def kernel(
    gxn,
    gyn,
    owners,
    rows_x,
    rows_y,
    depth,
    field_ref,
    class_ref,
    table_ref,
    forcing_ref,
    x_ref,
    y_ref,
    weight_ref,
    mixing_ref,
    proj_in,
    residual_ref,
    grad_ref,
    spec_ref,
    fwd_ref,
    inv_ref,
    send_ref,
    recv_ref,
    out_ref,
    gout_ref,
    slope_ref,
    pre_ref,
    press_ref,
    coef_ref,
    pair_ref,
    half_ref,
    skew_ref,
    mix_ref,
    mix_t_ref,
    proj_ref,
    sum_ref,
    spread_ref,
    x_send,
    x_recv,
    y_send,
    y_recv,
    send_sem,
    recv_sem,
    halo_send,
    halo_recv,
):
    n = gxn * gyn
    gx = lax.axis_index("gx")
    gy = lax.axis_index("gy")
    core = gx % 2
    chips = n // 2
    chip = gx // 2 * gyn + gy
    apart = n // owners
    group = owners // 2
    own = core * group + chip // apart
    owner = chip % apart == 0
    cells = rows_x * rows_y
    width = depth * C
    block = 2 * KX * KY // owners
    half = block // 2
    per = LANES // depth
    span = rows_y * depth
    columns = owners * block

    def if_owner(body):
        if apart == 1:
            body()
        else:
            pl.when(owner)(body)

    def place(index):
        return (2 * (index // gyn) + core, index % gyn)

    sibling = (gx + 1 - 2 * core, gy)
    beside = gx - 1 + 2 * core
    has_beside = jnp.logical_and(beside >= 0, beside < gxn)
    barrier = pltpu.get_barrier_semaphore()

    def greet(k, carry):
        target = lax.rem(chip + k, chips)
        pl.semaphore_signal(barrier, inc=1, device_id=place(target), device_id_type=MESH)
        return carry

    lax.fori_loop(1, chips, greet, 0)
    pl.semaphore_signal(barrier, inc=1, device_id=sibling, device_id_type=MESH)

    @pl.when(has_beside)
    def _():
        pl.semaphore_signal(barrier, inc=1, device_id=(beside, gy), device_id_type=MESH)

    def chosen(shape, rule):
        row_at = lax.broadcasted_iota(jnp.int32, shape, 0)
        lane_at = lax.broadcasted_iota(jnp.int32, shape, 1)
        return rule(row_at, lane_at)

    def ones(shape, rule):
        return jnp.where(chosen(shape, rule), 1.0, 0.0).astype(BF16)

    def tables(which):
        shape = (LANES, columns)
        slot = lax.broadcasted_iota(jnp.int32, shape, 0)
        column = lax.broadcasted_iota(jnp.int32, shape, 1)
        mode = column // block * half + column % half
        first_mode = mode // KY + 2 * KX * which
        second_mode = mode % KY + 2 * KY * which
        imaginary = column % block >= half
        x_here = x_ref[pl.ds(pl.multiple_of(gx * rows_x, rows_x), rows_x), :]
        y_here = y_ref[pl.ds(pl.multiple_of(gy * rows_y, rows_y), rows_y), :]
        cosine = jnp.where(slot == first_mode, 1.0, 0.0)
        sine = jnp.where(slot == first_mode + KX, 1.0, 0.0)
        first = dot(x_here, jnp.where(imaginary, sine, cosine).astype(BF16))
        second = dot(x_here, jnp.where(imaginary, -cosine, sine).astype(BF16))
        fine = slot % (LANES // 2)
        y_cos = dot(y_here, jnp.where(fine == second_mode, 1.0, 0.0).astype(BF16))
        y_sin = dot(y_here, jnp.where(fine == second_mode + KY, 1.0, 0.0).astype(BF16))
        return first, second, y_cos, y_sin

    def fill(which, ref):
        first, second, y_cos, y_sin = tables(which)
        for x in range(rows_x):
            made = first[x : x + 1] * y_cos + second[x : x + 1] * y_sin
            ref[x * rows_y : (x + 1) * rows_y, :] = made.astype(BF16)

    fill(0, fwd_ref)
    pl.semaphore_wait(barrier, chips + jnp.where(has_beside, 1, 0))

    classes = class_ref[...]
    perm = jnp.zeros(classes.shape, F32)
    for level in range(CLASSES):
        perm = jnp.where(classes == level, table_ref[level], perm)

    sides = (
        (gx > 0, (gx - 1, gy), x_send, x_recv, 0),
        (gx < gxn - 1, (gx + 1, gy), x_send, x_recv, 1),
        (gy > 0, (gx, gy - 1), y_send, y_recv, 0),
        (gy < gyn - 1, (gx, gy + 1), y_send, y_recv, 1),
    )

    def halo_copy(turn, side):
        _, target, source, landing, end = sides[side]
        return pltpu.make_async_remote_copy(
            src_ref=source.at[turn, end],
            dst_ref=landing.at[turn, 1 - end],
            send_sem=halo_send.at[turn, side],
            recv_sem=halo_recv.at[turn, side ^ 1],
            device_id=target,
            device_id_type=MESH,
        )

    def halo_start(turn, value):
        x_send[turn, 0] = value[0:1, :]
        x_send[turn, 1] = value[rows_x - 1 : rows_x, :]
        y_send[turn, 0] = value[:, 0:LANES]
        y_send[turn, 1] = value[:, span - LANES : span]
        for side in range(4):
            there, _, _, landing, end = sides[side]

            @pl.when(there)
            def _():
                halo_copy(turn, side).start()

            @pl.when(jnp.logical_not(there))
            def _():
                landing[turn, end] = jnp.zeros(landing.shape[2:], F32)

    def halo_wait(turn):
        for side in range(4):
            there, _, _, landing, end = sides[side]

            @pl.when(there)
            def _():
                copy = halo_copy(turn, side)
                copy.wait_send()
                pltpu.make_async_copy(
                    landing.at[turn, end], landing.at[turn, end], halo_recv.at[turn, side]
                ).wait()

    row = lax.broadcasted_iota(jnp.int32, (rows_x, span), 0)
    layer = lane_iota((rows_x, span)) % depth
    lane = lane_iota((rows_x, LANES))

    def neighbours(turn, value):
        below = jnp.where(row == 0, x_recv[turn, 0], pltpu.roll(value, 1, 0))
        above = jnp.where(row == rows_x - 1, x_recv[turn, 1], pltpu.roll(value, rows_x - 1, 0))
        moved = pltpu.roll(value, depth, 1)
        edge = jnp.where(lane < depth, pltpu.roll(y_recv[turn, 0], depth, 1), moved[:, :LANES])
        left = jnp.concatenate([edge, moved[:, LANES:]], axis=1)
        moved = pltpu.roll(value, span - depth, 1)
        edge = jnp.where(
            lane >= LANES - depth,
            pltpu.roll(y_recv[turn, 1], LANES - depth, 1),
            moved[:, span - LANES :],
        )
        right = jnp.concatenate([moved[:, : span - LANES], edge], axis=1)
        under = jnp.where(layer == 0, 0.0, pltpu.roll(value, 1, 1))
        over = jnp.where(layer == depth - 1, 0.0, pltpu.roll(value, span - 1, 1))
        return (below, above, left, right, under, over)

    halo_start(0, perm)

    def to_sibling(source, landing, sem):
        return pltpu.make_async_remote_copy(
            src_ref=source,
            dst_ref=landing,
            send_sem=send_sem.at[sem],
            recv_sem=recv_sem.at[sem],
            device_id=sibling,
            device_id_type=MESH,
        )

    def wait_chunks(ref, count, sem):
        held = ref.shape[0]
        for _ in range(count // held):
            pltpu.make_async_copy(ref, ref, sem).wait()
        if count % held:
            rest = ref.at[pl.ds(0, count % held)]
            pltpu.make_async_copy(rest, rest, sem).wait()

    def wait_owned(ref, sem):
        some = ref.at[pl.ds(0, group)]
        if_owner(lambda: wait_chunks(some, group - 1, sem))
        if apart > 1:
            pl.when(jnp.logical_not(owner))(lambda: wait_chunks(some, group, sem))

    mine = pl.ds(core * group, group)
    theirs = pl.ds((1 - core) * group, group)

    def all_to_all(phase, right_ref, table):
        lanes = group * block

        def product(which):
            start = pl.multiple_of(which * lanes, lanes)
            return dot_first(table[:, pl.ds(start, lanes)], right_ref[...])

        send_ref[theirs] = product(1 - core).astype(BF16).reshape(group, block, width)
        pair = to_sibling(send_ref.at[theirs], pair_ref.at[phase], 4 * phase)
        pair.start()
        half_ref[...] = product(core)
        pair.wait()
        total = half_ref[...] + pair_ref[phase].reshape(lanes, width).astype(F32)
        send_ref[mine] = total.astype(BF16).reshape(group, block, width)

        def push(k, carry):
            target = k * apart

            @pl.when(target != chip)
            def _():
                pltpu.make_async_remote_copy(
                    src_ref=send_ref.at[core * group + k],
                    dst_ref=recv_ref.at[phase, chip],
                    send_sem=send_sem.at[4 * phase + 1],
                    recv_sem=recv_sem.at[4 * phase + 1],
                    device_id=place(target),
                    device_id_type=MESH,
                ).start()

            return carry

        lax.fori_loop(0, group, push, 0)

    def all_to_all_sum(phase):
        recv_ref[phase, chip] = send_ref[own]
        wait_chunks(recv_ref.at[phase], chips - 1, recv_sem.at[4 * phase + 1])

        def body(k, total):
            return total + recv_ref[phase, k].astype(F32)

        total = lax.fori_loop(0, chips, body, jnp.zeros((block, width), F32))

        def lines(part):
            return jnp.concatenate(
                [part[:, k : k + LANES] for k in range(0, width, LANES)], axis=0
            )

        return lines(total[:half]), lines(total[half:])

    parts = width // LANES

    def unlines(part):
        return jnp.concatenate([part[k * half : (k + 1) * half] for k in range(parts)], axis=1)

    def weights(shift):
        real = jnp.concatenate([skew_ref[shift, :half]] * parts, axis=0)
        imaginary = jnp.concatenate([skew_ref[shift, half:]] * parts, axis=0)
        return real, imaginary

    def all_gather(phase, ref):
        def push(k, carry):
            target = lax.rem(chip + k, chips)
            pltpu.make_async_remote_copy(
                src_ref=ref.at[own],
                dst_ref=ref.at[own],
                send_sem=send_sem.at[4 * phase + 2],
                recv_sem=recv_sem.at[4 * phase + 2],
                device_id=place(target),
                device_id_type=MESH,
            ).start()
            return carry

        lax.fori_loop(1, chips, push, 0)

    def all_gather_wait(phase, ref):
        wait_owned(ref, recv_sem.at[4 * phase + 2])
        pair = to_sibling(ref.at[mine], ref.at[mine], 4 * phase + 3)
        pair.start()
        pair.wait()
        if_owner(
            lambda: wait_chunks(ref.at[pl.ds(0, group)], chips - 1, send_sem.at[4 * phase + 2])
        )
        wait_owned(send_ref, send_sem.at[4 * phase + 1])

    all_to_all(0, field_ref, fwd_ref)
    fill(1, inv_ref)
    step = mix_ref.shape[0]
    repeat = ones((step, C), lambda r, l: r % C == l)
    repeat_t = ones((C, step), lambda r, l: r == l % C)
    blocks = chosen((step, step), lambda r, l: r // C == l // C)
    tall = dot(repeat, mixing_ref[...]).astype(BF16)
    mix_ref[...] = jnp.where(blocks, dot(tall, repeat_t), 0.0).astype(BF16)
    tall = lax.dot_general(
        repeat, mixing_ref[...], (((1,), (1,)), ((), ())), preferred_element_type=F32
    ).astype(BF16)
    mix_t_ref[...] = jnp.where(blocks, dot(tall, repeat_t), 0.0).astype(BF16)
    sum_ref[...] = ones(sum_ref.shape, lambda r, l: r // C == l % depth)
    spread_ref[...] = ones(spread_ref.shape, lambda r, l: l // C == r % depth)
    channel = lane_iota((1, width)) % C
    proj_row = jnp.zeros((1, width), F32)
    for k in range(C):
        proj_row = jnp.where(channel == k, proj_in[k], proj_row)
    proj_ref[...] = proj_row
    for shift in range(C):
        pick = ones(
            (C * C, LANES),
            lambda r, l: (r % C == l % C) & (r // C == (l % C - shift + C) % C),
        )
        skew_ref[shift] = dot(weight_ref[...], pick)

    @if_owner
    def _():
        real, imaginary = all_to_all_sum(0)
        coef_ref[0] = real
        coef_ref[1] = imaginary
        out_real = jnp.zeros_like(real)
        out_imag = jnp.zeros_like(real)
        for shift in range(C):
            w_real, w_imag = weights(shift)
            c_real = group_roll(real, shift)
            c_imag = group_roll(imaginary, shift)
            out_real = out_real + (c_real * w_real - c_imag * w_imag)
            out_imag = out_imag + (c_real * w_imag + c_imag * w_real)
        mixed = jnp.concatenate([unlines(out_real), unlines(out_imag)], axis=0)
        out_ref[own] = mixed.astype(BF16)
        all_gather(0, out_ref)

    all_gather_wait(0, out_ref)

    chunk = 4 * rows_y

    def local(value, matrix):
        return jnp.concatenate(
            [dot(value[:, k : k + step], matrix) for k in range(0, width, step)], axis=1
        )

    def activate(index, carry):
        here = pl.ds(pl.multiple_of(index * chunk, chunk), chunk)
        spectral = dot(inv_ref[here, :], out_ref[...].reshape(columns, width))
        preact = spectral.astype(BF16).astype(F32) + local(field_ref[here, :], mix_ref[...])
        bell = 0.5 * (1.0 + lax.erf(preact * ROOT_HALF))
        tail = preact * jnp.exp(-0.5 * preact * preact) * INV_ROOT_TWO_PI
        slope_ref[here, :] = (bell + tail) * proj_ref[...]
        press_ref[here, :] = split_dot(preact * bell * proj_ref[...], sum_ref[...])
        return carry

    lax.fori_loop(0, cells // chunk, activate, 0)

    def gathered(index):
        made = press_ref[pl.ds(index * per, rows_x, stride=rows_y), :]
        for k in range(1, per):
            other = press_ref[pl.ds(index * per + k, rows_x, stride=rows_y), :]
            made = jnp.where(lane // depth == k, other, made)
        return made

    pressure = jnp.concatenate([gathered(k) for k in range(rows_y // per)], axis=1)
    halo_start(1, pressure)
    halo_wait(0)
    means = [0.5 * (perm + other) for other in neighbours(0, perm)]
    halo_wait(1)

    def operator(turn, value):
        total = jnp.zeros_like(value)
        for mean, other in zip(means, neighbours(turn, value)):
            total = total + mean * (value - other)
        return total

    residual = operator(1, pressure) - forcing_ref[...]
    residual_ref[...] = residual
    halo_start(2, residual)
    halo_wait(2)
    slope_source = operator(2, residual)
    for k in range(rows_y // per):
        piece = slope_source[:, k * LANES : (k + 1) * LANES]
        for j in range(per):
            press_ref[pl.ds(k * per + j, rows_x, stride=rows_y), :] = jnp.where(
                lane // depth == j, piece, 0.0
            )

    def differentiate(index, carry):
        here = pl.ds(pl.multiple_of(index * chunk, chunk), chunk)
        wide = split_dot(press_ref[here, :], spread_ref[...])
        pre_ref[here, :] = (wide * slope_ref[here, :]).astype(BF16)
        return carry

    lax.fori_loop(0, cells // chunk, differentiate, 0)

    all_to_all(1, pre_ref, inv_ref)

    @if_owner
    def _():
        g_real, g_imag = all_to_all_sum(1)
        real = coef_ref[0]
        imaginary = coef_ref[1]
        in_real = jnp.zeros_like(real)
        in_imag = jnp.zeros_like(real)
        grads = [[jnp.zeros((half, LANES), F32) for _ in range(C * C // LANES)] for _ in range(2)]
        spot = lane_iota((half, LANES))
        for shift in range(C):
            w_real, w_imag = weights(shift)
            in_real = in_real + group_roll(g_real * w_real + g_imag * w_imag, (C - shift) % C)
            in_imag = in_imag + group_roll(g_imag * w_real - g_real * w_imag, (C - shift) % C)
            c_real = group_roll(real, shift)
            c_imag = group_roll(imaginary, shift)
            both = (c_real * g_real + c_imag * g_imag, c_real * g_imag - c_imag * g_real)
            for which in range(2):
                total = both[which][:half]
                for k in range(1, parts):
                    total = total + both[which][k * half : (k + 1) * half]
                turn = C
                while turn < LANES:
                    total = total + pltpu.roll(total, turn, 1)
                    turn *= 2
                for k in range(C * C // LANES):
                    source = k * (LANES // C) + spot // C
                    match = (spot % C - source + C) % C == shift
                    grads[which][k] = jnp.where(match, total, grads[which][k])
        message = jnp.concatenate(
            [
                jnp.concatenate([unlines(in_real)] + grads[0], axis=1),
                jnp.concatenate([unlines(in_imag)] + grads[1], axis=1),
            ],
            axis=0,
        )
        gout_ref[own] = message.astype(BF16)
        all_gather(1, gout_ref)

    all_gather_wait(1, gout_ref)

    def finish(index, carry):
        here = pl.ds(pl.multiple_of(index * chunk, chunk), chunk)
        spectral = dot(fwd_ref[here, :], gout_ref[:, :, :width].reshape(columns, width))
        total = spectral.astype(BF16).astype(F32) + local(pre_ref[here, :], mix_t_ref[...])
        grad_ref[here, :] = total.astype(BF16)
        return carry

    lax.fori_loop(0, cells // chunk, finish, 0)

    def report(k, carry):
        terms = gout_ref[k, :, width:].astype(F32)
        spec_ref[0, k] = terms[:half]
        spec_ref[1, k] = terms[half:]
        return carry

    lax.fori_loop(0, owners, report, 0)


def angle_tables(length, count, scale):
    frequencies = np.arange(count) - count // 2
    turns = np.arange(length)[:, None] * frequencies[None, :] % length
    angle = turns.astype(np.float32) * np.float32(2.0 * math.pi / length)
    return np.cos(angle) * np.float32(scale), np.sin(angle) * np.float32(scale)


def x_table(length):
    parts = []
    for scale in (1.0 / math.sqrt(length), 1.0 / math.sqrt(KX)):
        cosine, sine = angle_tables(length, KX, scale)
        parts += [cosine, -sine]
    table = np.concatenate(parts, axis=1)
    return np.pad(table, ((0, 0), (0, LANES - table.shape[1]))).astype(BF16)


def y_table(length):
    parts = []
    for scale in (1.0 / math.sqrt(length), 1.0 / math.sqrt(KY)):
        parts += list(angle_tables(length, KY, scale))
    table = np.concatenate(parts, axis=1)
    high = table.astype(BF16)
    low = (table - high.astype(np.float32)).astype(BF16)
    return np.concatenate([high, low], axis=1)


def shards(field, perm_class, perm_table, forcing, spec_weight, mix_weight, proj):
    gxn = lax.axis_size("gx")
    gyn = lax.axis_size("gy")
    n = gxn * gyn
    gx = lax.axis_index("gx")
    gy = lax.axis_index("gy")
    rows_x, rows_y, width = field.shape
    depth = width // C
    cells = rows_x * rows_y
    span_x = rows_x * gxn
    span_y = rows_y * gyn
    owners = min(n, KX * KY // 8)
    modes = KX * KY // owners
    block = 2 * modes
    columns = owners * block
    own = gx % 2 * (owners // 2) + (gx // 2 * gyn + gy) // (n // owners)
    weights = lax.dynamic_slice_in_dim(
        spec_weight.reshape(2, KX * KY, C, C), own * modes, modes, 1
    ).reshape(block, C * C)
    step = min(256, width)

    vmem = pl.BlockSpec(memory_space=pltpu.VMEM)
    smem = pl.BlockSpec(memory_space=pltpu.SMEM)
    residual, grad_field, spec = pl.pallas_call(
        functools.partial(kernel, gxn, gyn, owners, rows_x, rows_y, depth),
        out_shape=(
            jax.ShapeDtypeStruct((rows_x, rows_y * depth), F32),
            jax.ShapeDtypeStruct((cells, width), BF16),
            jax.ShapeDtypeStruct((2, owners, modes, C * C), F32),
        ),
        in_specs=[vmem, vmem, smem] + [vmem] * 5 + [smem],
        out_specs=(vmem, vmem, vmem),
        scratch_shapes=[
            pltpu.VMEM((cells, columns), BF16),
            pltpu.VMEM((cells, columns), BF16),
            pltpu.VMEM((owners, block, width), BF16),
            pltpu.VMEM((2, n // 2, block, width), BF16),
            pltpu.VMEM((owners, block, width), BF16),
            pltpu.VMEM((owners, block, width + C * C), BF16),
            pltpu.VMEM((cells, width), F32),
            pltpu.VMEM((cells, width), BF16),
            pltpu.VMEM((cells, LANES), F32),
            pltpu.VMEM((2, modes * width // LANES, LANES), F32),
            pltpu.VMEM((2, owners // 2, block, width), BF16),
            pltpu.VMEM((columns // 2, width), F32),
            pltpu.VMEM((C, block, LANES), F32),
            pltpu.VMEM((step, step), BF16),
            pltpu.VMEM((step, step), BF16),
            pltpu.VMEM((1, width), F32),
            pltpu.VMEM((width, LANES), BF16),
            pltpu.VMEM((LANES, width), BF16),
            pltpu.VMEM((3, 2, 1, rows_y * depth), F32),
            pltpu.VMEM((3, 2, 1, rows_y * depth), F32),
            pltpu.VMEM((3, 2, rows_x, LANES), F32),
            pltpu.VMEM((3, 2, rows_x, LANES), F32),
            pltpu.SemaphoreType.DMA((8,)),
            pltpu.SemaphoreType.DMA((8,)),
            pltpu.SemaphoreType.DMA((3, 4)),
            pltpu.SemaphoreType.DMA((3, 4)),
        ],
        compiler_params=pltpu.CompilerParams(
            collective_id=0, has_side_effects=True, vmem_limit_bytes=60 * 1024 * 1024
        ),
        name="fourier_darcy",
    )(
        field.reshape(cells, width),
        perm_class,
        perm_table,
        forcing,
        jnp.asarray(x_table(span_x)),
        jnp.asarray(y_table(span_y)),
        weights,
        mix_weight,
        proj,
    )
    spec_grad = spec.reshape(2, KX, KY, C, C)
    return (residual, grad_field.reshape(rows_x, rows_y, width), spec_grad)


def solution(mesh):
    placed = (P("gx", "gy", None), P("gx", "gy"), P(), P("gx", "gy"), P(), P(), P())
    return jax.shard_map(
        shards,
        mesh=mesh,
        in_specs=placed,
        out_specs=(P("gx", "gy"), P("gx", "gy", None), P()),
        check_vma=False,
    )
```

```python
import functools
import math

import jax
import jax.numpy as jnp
import numpy as np
from jax import lax
from jax.experimental import pallas as pl
from jax.experimental.pallas import tpu as pltpu
from jax.sharding import PartitionSpec as P

C = 16
KX = 16
KY = 16
CLASSES = 8
LANES = 128
HALVES = 2
ROOT_HALF = 0.7071067811865476
INV_ROOT_TWO_PI = 0.3989422804014327
MESH = pl.DeviceIdType.MESH
F32 = jnp.float32
BF16 = jnp.bfloat16


def dot(left, right):
    return jnp.dot(left, right, preferred_element_type=F32)


def dot_first(left, right):
    return lax.dot_general(left, right, (((0,), (0,)), ((), ())), preferred_element_type=F32)


def split_dot(value, right):
    high = value.astype(BF16)
    low = (value - high.astype(F32)).astype(BF16)
    return dot(high, right) + dot(low, right)


def lane_iota(shape):
    return lax.broadcasted_iota(jnp.int32, shape, len(shape) - 1)


def group_roll(value, amount):
    if amount == 0:
        return value
    inside = lane_iota(value.shape) % C >= amount
    return jnp.where(
        inside, pltpu.roll(value, amount, 1), pltpu.roll(value, LANES - C + amount, 1)
    )


def kernel(
    gxn,
    gyn,
    owners,
    rows_x,
    rows_y,
    depth,
    field_ref,
    class_ref,
    table_ref,
    forcing_ref,
    x_ref,
    y_ref,
    weight_ref,
    mixing_ref,
    proj_in,
    residual_ref,
    grad_ref,
    spec_ref,
    fwd_ref,
    inv_ref,
    send_ref,
    recv_ref,
    out_ref,
    gout_ref,
    terms_ref,
    total_ref,
    slope_ref,
    pre_ref,
    press_ref,
    coef_ref,
    pair_ref,
    half_ref,
    skew_ref,
    mix_ref,
    mix_t_ref,
    proj_ref,
    sum_ref,
    spread_ref,
    x_send,
    x_recv,
    y_send,
    y_recv,
    send_sem,
    recv_sem,
    halo_send,
    halo_recv,
):
    n = gxn * gyn
    gx = lax.axis_index("gx")
    gy = lax.axis_index("gy")
    core = gx % 2
    chips = n // 2
    chip = gx // 2 * gyn + gy
    apart = n // owners
    group = owners // 2
    own = core * group + chip // apart
    owner = chip % apart == 0
    cells = rows_x * rows_y
    width = depth * C
    block = 2 * KX * KY // owners
    half = block // 2
    per = LANES // depth
    span = rows_y * depth
    wide = width // HALVES
    parts = wide // LANES
    columns = owners * block

    def if_owner(body):
        if apart == 1:
            body()
        else:
            pl.when(owner)(body)

    def place(index):
        return (2 * (index // gyn) + core, index % gyn)

    sibling = (gx + 1 - 2 * core, gy)
    beside = gx - 1 + 2 * core
    has_beside = jnp.logical_and(beside >= 0, beside < gxn)
    barrier = pltpu.get_barrier_semaphore()

    def greet(k, carry):
        target = lax.rem(chip + k, chips)
        pl.semaphore_signal(barrier, inc=1, device_id=place(target), device_id_type=MESH)
        return carry

    lax.fori_loop(1, chips, greet, 0)
    pl.semaphore_signal(barrier, inc=1, device_id=sibling, device_id_type=MESH)

    @pl.when(has_beside)
    def _():
        pl.semaphore_signal(barrier, inc=1, device_id=(beside, gy), device_id_type=MESH)

    def chosen(shape, rule):
        row_at = lax.broadcasted_iota(jnp.int32, shape, 0)
        lane_at = lax.broadcasted_iota(jnp.int32, shape, 1)
        return rule(row_at, lane_at)

    def ones(shape, rule):
        return jnp.where(chosen(shape, rule), 1.0, 0.0).astype(BF16)

    def tables(which):
        shape = (LANES, columns)
        slot = lax.broadcasted_iota(jnp.int32, shape, 0)
        column = lax.broadcasted_iota(jnp.int32, shape, 1)
        mode = column // block * half + column % half
        first_mode = mode // KY + 2 * KX * which
        second_mode = mode % KY + 2 * KY * which
        imaginary = column % block >= half
        x_here = x_ref[pl.ds(pl.multiple_of(gx * rows_x, rows_x), rows_x), :]
        y_here = y_ref[pl.ds(pl.multiple_of(gy * rows_y, rows_y), rows_y), :]
        cosine = jnp.where(slot == first_mode, 1.0, 0.0)
        sine = jnp.where(slot == first_mode + KX, 1.0, 0.0)
        first = dot(x_here, jnp.where(imaginary, sine, cosine).astype(BF16))
        second = dot(x_here, jnp.where(imaginary, -cosine, sine).astype(BF16))
        fine = slot % (LANES // 2)
        y_cos = dot(y_here, jnp.where(fine == second_mode, 1.0, 0.0).astype(BF16))
        y_sin = dot(y_here, jnp.where(fine == second_mode + KY, 1.0, 0.0).astype(BF16))
        return first, second, y_cos, y_sin

    def fill(which, ref):
        first, second, y_cos, y_sin = tables(which)
        for x in range(rows_x):
            made = first[x : x + 1] * y_cos + second[x : x + 1] * y_sin
            ref[x * rows_y : (x + 1) * rows_y, :] = made.astype(BF16)

    fill(0, fwd_ref)
    pl.semaphore_wait(barrier, chips + jnp.where(has_beside, 1, 0))

    classes = class_ref[...]
    perm = jnp.zeros(classes.shape, F32)
    for level in range(CLASSES):
        perm = jnp.where(classes == level, table_ref[level], perm)

    sides = (
        (gx > 0, (gx - 1, gy), x_send, x_recv, 0),
        (gx < gxn - 1, (gx + 1, gy), x_send, x_recv, 1),
        (gy > 0, (gx, gy - 1), y_send, y_recv, 0),
        (gy < gyn - 1, (gx, gy + 1), y_send, y_recv, 1),
    )

    def halo_copy(turn, side):
        _, target, source, landing, end = sides[side]
        return pltpu.make_async_remote_copy(
            src_ref=source.at[turn, end],
            dst_ref=landing.at[turn, 1 - end],
            send_sem=halo_send.at[turn, side],
            recv_sem=halo_recv.at[turn, side ^ 1],
            device_id=target,
            device_id_type=MESH,
        )

    def halo_start(turn, value):
        x_send[turn, 0] = value[0:1, :]
        x_send[turn, 1] = value[rows_x - 1 : rows_x, :]
        y_send[turn, 0] = value[:, 0:LANES]
        y_send[turn, 1] = value[:, span - LANES : span]
        for side in range(4):
            there, _, _, landing, end = sides[side]

            @pl.when(there)
            def _():
                halo_copy(turn, side).start()

            @pl.when(jnp.logical_not(there))
            def _():
                landing[turn, end] = jnp.zeros(landing.shape[2:], F32)

    def halo_wait(turn):
        for side in range(4):
            there, _, _, landing, end = sides[side]

            @pl.when(there)
            def _():
                copy = halo_copy(turn, side)
                copy.wait_send()
                pltpu.make_async_copy(
                    landing.at[turn, end], landing.at[turn, end], halo_recv.at[turn, side]
                ).wait()

    row = lax.broadcasted_iota(jnp.int32, (rows_x, span), 0)
    layer = lane_iota((rows_x, span)) % depth
    lane = lane_iota((rows_x, LANES))

    def neighbours(turn, value):
        below = jnp.where(row == 0, x_recv[turn, 0], pltpu.roll(value, 1, 0))
        above = jnp.where(row == rows_x - 1, x_recv[turn, 1], pltpu.roll(value, rows_x - 1, 0))
        moved = pltpu.roll(value, depth, 1)
        edge = jnp.where(lane < depth, pltpu.roll(y_recv[turn, 0], depth, 1), moved[:, :LANES])
        left = jnp.concatenate([edge, moved[:, LANES:]], axis=1)
        moved = pltpu.roll(value, span - depth, 1)
        edge = jnp.where(
            lane >= LANES - depth,
            pltpu.roll(y_recv[turn, 1], LANES - depth, 1),
            moved[:, span - LANES :],
        )
        right = jnp.concatenate([moved[:, : span - LANES], edge], axis=1)
        under = jnp.where(layer == 0, 0.0, pltpu.roll(value, 1, 1))
        over = jnp.where(layer == depth - 1, 0.0, pltpu.roll(value, span - 1, 1))
        return (below, above, left, right, under, over)

    halo_start(0, perm)

    def to_sibling(source, landing, sem):
        return pltpu.make_async_remote_copy(
            src_ref=source,
            dst_ref=landing,
            send_sem=send_sem.at[sem],
            recv_sem=recv_sem.at[sem],
            device_id=sibling,
            device_id_type=MESH,
        )

    def wait_chunks(ref, count, sem):
        held = ref.shape[0]
        for _ in range(count // held):
            pltpu.make_async_copy(ref, ref, sem).wait()
        if count % held:
            rest = ref.at[pl.ds(0, count % held)]
            pltpu.make_async_copy(rest, rest, sem).wait()

    def wait_owned(ref, sem):
        some = ref.at[pl.ds(0, group)]
        if_owner(lambda: wait_chunks(some, group - 1, sem))
        if apart > 1:
            pl.when(jnp.logical_not(owner))(lambda: wait_chunks(some, group, sem))

    mine = pl.ds(core * group, group)
    theirs = pl.ds((1 - core) * group, group)

    lanes = group * block

    def sem(phase, piece, stage):
        return (phase * HALVES + piece) * 4 + stage

    def strip(piece):
        return slice(piece * wide, (piece + 1) * wide)

    def product(which, piece, right_ref, table):
        start = pl.multiple_of(which * lanes, lanes)
        return dot_first(table[:, pl.ds(start, lanes)], right_ref[:, strip(piece)])

    def pair_copy(phase, piece):
        return to_sibling(
            send_ref.at[piece, theirs], pair_ref.at[phase, piece], sem(phase, piece, 0)
        )

    def give(phase, piece, right_ref, table):
        made = product(1 - core, piece, right_ref, table)
        send_ref[piece, theirs] = made.astype(BF16).reshape(group, block, wide)
        pair_copy(phase, piece).start()

    def keep(piece, right_ref, table):
        half_ref[piece] = product(core, piece, right_ref, table)

    def send(phase, piece):
        pair_copy(phase, piece).wait()
        total = half_ref[piece] + pair_ref[phase, piece].reshape(lanes, wide).astype(F32)
        send_ref[piece, mine] = total.astype(BF16).reshape(group, block, wide)

        def push(k, carry):
            target = k * apart

            @pl.when(target != chip)
            def _():
                pltpu.make_async_remote_copy(
                    src_ref=send_ref.at[piece, core * group + k],
                    dst_ref=recv_ref.at[phase, piece, chip],
                    send_sem=send_sem.at[sem(phase, piece, 1)],
                    recv_sem=recv_sem.at[sem(phase, piece, 1)],
                    device_id=place(target),
                    device_id_type=MESH,
                ).start()

            return carry

        lax.fori_loop(0, group, push, 0)

    def collect(phase, piece):
        recv_ref[phase, piece, chip] = send_ref[piece, own]
        wait_chunks(recv_ref.at[phase, piece], chips - 1, recv_sem.at[sem(phase, piece, 1)])

        def body(k, total):
            return total + recv_ref[phase, piece, k].astype(F32)

        total = lax.fori_loop(0, chips, body, jnp.zeros((block, wide), F32))

        def lines(part):
            return jnp.concatenate([part[:, k : k + LANES] for k in range(0, wide, LANES)], axis=0)

        return lines(total[:half]), lines(total[half:])

    def unlines(part):
        return jnp.concatenate([part[k * half : (k + 1) * half] for k in range(parts)], axis=1)

    def weights(shift):
        real = jnp.concatenate([skew_ref[shift, :half]] * parts, axis=0)
        imaginary = jnp.concatenate([skew_ref[shift, half:]] * parts, axis=0)
        return real, imaginary

    def gather_push(ref, at):
        def push(k, carry):
            target = lax.rem(chip + k, chips)
            pltpu.make_async_remote_copy(
                src_ref=ref.at[own],
                dst_ref=ref.at[own],
                send_sem=send_sem.at[at],
                recv_sem=recv_sem.at[at],
                device_id=place(target),
                device_id_type=MESH,
            ).start()
            return carry

        lax.fori_loop(1, chips, push, 0)

    def gather_pass(ref, at):
        wait_owned(ref, recv_sem.at[at])
        to_sibling(ref.at[mine], ref.at[mine], at + 1).start()

    def gather_wait(ref, at):
        to_sibling(ref.at[mine], ref.at[mine], at + 1).wait()

    def gather_end(ref, at):
        if_owner(lambda: wait_chunks(ref.at[pl.ds(0, group)], chips - 1, send_sem.at[at]))

    give(0, 0, field_ref, fwd_ref)
    keep(0, field_ref, fwd_ref)
    give(0, 1, field_ref, fwd_ref)
    send(0, 0)
    keep(1, field_ref, fwd_ref)
    send(0, 1)

    fill(1, inv_ref)
    step = mix_ref.shape[0]
    repeat = ones((step, C), lambda r, l: r % C == l)
    repeat_t = ones((C, step), lambda r, l: r == l % C)
    blocks = chosen((step, step), lambda r, l: r // C == l // C)
    tall = dot(repeat, mixing_ref[...]).astype(BF16)
    mix_ref[...] = jnp.where(blocks, dot(tall, repeat_t), 0.0).astype(BF16)
    tall = lax.dot_general(
        repeat, mixing_ref[...], (((1,), (1,)), ((), ())), preferred_element_type=F32
    ).astype(BF16)
    mix_t_ref[...] = jnp.where(blocks, dot(tall, repeat_t), 0.0).astype(BF16)
    sum_ref[...] = ones(sum_ref.shape, lambda r, l: r // C == l % depth)
    spread_ref[...] = ones(spread_ref.shape, lambda r, l: l // C == r % depth)
    channel = lane_iota((1, width)) % C
    proj_row = jnp.zeros((1, width), F32)
    for k in range(C):
        proj_row = jnp.where(channel == k, proj_in[k], proj_row)
    proj_ref[...] = proj_row
    for shift in range(C):
        pick = ones(
            (C * C, LANES),
            lambda r, l: (r % C == l % C) & (r // C == (l % C - shift + C) % C),
        )
        skew_ref[shift] = dot(weight_ref[...], pick)

    def mix(piece):
        real, imaginary = collect(0, piece)
        coef_ref[piece, 0] = real
        coef_ref[piece, 1] = imaginary
        out_real = jnp.zeros_like(real)
        out_imag = jnp.zeros_like(real)
        for shift in range(C):
            w_real, w_imag = weights(shift)
            c_real = group_roll(real, shift)
            c_imag = group_roll(imaginary, shift)
            out_real = out_real + (c_real * w_real - c_imag * w_imag)
            out_imag = out_imag + (c_real * w_imag + c_imag * w_real)
        mixed = jnp.concatenate([unlines(out_real), unlines(out_imag)], axis=0)
        out_ref[piece, own] = mixed.astype(BF16)
        gather_push(out_ref.at[piece], sem(0, piece, 2))

    for piece in range(HALVES):
        if_owner(functools.partial(mix, piece))

    chunk = 4 * rows_y
    steps = cells // chunk

    def activate(piece, index, carry):
        here = pl.ds(pl.multiple_of(index * chunk, chunk), chunk)
        part = strip(piece)
        spectral = dot(inv_ref[here, :], out_ref[piece].reshape(columns, wide))
        preact = spectral.astype(BF16).astype(F32) + dot(field_ref[here, part], mix_ref[...])
        bell = 0.5 * (1.0 + lax.erf(preact * ROOT_HALF))
        tail = preact * jnp.exp(-0.5 * preact * preact) * INV_ROOT_TWO_PI
        row_proj = proj_ref[:, part]
        slope_ref[here, part] = (bell + tail) * row_proj
        share = split_dot(preact * bell * row_proj, sum_ref[part, :])
        press_ref[here, :] = share if piece == 0 else press_ref[here, :] + share
        return carry

    def staged(phase, ref, work):
        gather_pass(ref.at[0], sem(phase, 0, 2))
        gather_wait(ref.at[0], sem(phase, 0, 2))
        lax.fori_loop(0, steps // 2, functools.partial(work, 0), 0)
        gather_pass(ref.at[1], sem(phase, 1, 2))
        lax.fori_loop(steps // 2, steps, functools.partial(work, 0), 0)
        gather_wait(ref.at[1], sem(phase, 1, 2))
        lax.fori_loop(0, steps, functools.partial(work, 1), 0)

    def end_sends(phase, ref):
        for piece in range(HALVES):
            gather_end(ref.at[piece], sem(phase, piece, 2))
            wait_owned(send_ref.at[piece], send_sem.at[sem(phase, piece, 1)])

    staged(0, out_ref, activate)

    def gathered(index):
        made = press_ref[pl.ds(index * per, rows_x, stride=rows_y), :]
        for k in range(1, per):
            other = press_ref[pl.ds(index * per + k, rows_x, stride=rows_y), :]
            made = jnp.where(lane // depth == k, other, made)
        return made

    end_sends(0, out_ref)
    pressure = jnp.concatenate([gathered(k) for k in range(rows_y // per)], axis=1)
    halo_start(1, pressure)
    halo_wait(0)
    means = [0.5 * (perm + other) for other in neighbours(0, perm)]
    halo_wait(1)

    def operator(turn, value):
        total = jnp.zeros_like(value)
        for mean, other in zip(means, neighbours(turn, value)):
            total = total + mean * (value - other)
        return total

    residual = operator(1, pressure) - forcing_ref[...]
    residual_ref[...] = residual
    halo_start(2, residual)
    halo_wait(2)
    slope_source = operator(2, residual)
    for k in range(rows_y // per):
        piece = slope_source[:, k * LANES : (k + 1) * LANES]
        for j in range(per):
            press_ref[pl.ds(k * per + j, rows_x, stride=rows_y), :] = jnp.where(
                lane // depth == j, piece, 0.0
            )

    def differentiate(piece, index, carry):
        here = pl.ds(pl.multiple_of(index * chunk, chunk), chunk)
        part = strip(piece)
        source = split_dot(press_ref[here, :], spread_ref[:, part])
        pre_ref[here, part] = (source * slope_ref[here, part]).astype(BF16)
        return carry

    lax.fori_loop(0, steps, functools.partial(differentiate, 0), 0)
    give(1, 0, pre_ref, inv_ref)
    keep(0, pre_ref, inv_ref)
    lax.fori_loop(0, steps, functools.partial(differentiate, 1), 0)
    send(1, 0)
    give(1, 1, pre_ref, inv_ref)
    keep(1, pre_ref, inv_ref)
    send(1, 1)

    def mix_back(piece):
        g_real, g_imag = collect(1, piece)
        real = coef_ref[piece, 0]
        imaginary = coef_ref[piece, 1]
        in_real = jnp.zeros_like(real)
        in_imag = jnp.zeros_like(real)
        for shift in range(C):
            w_real, w_imag = weights(shift)
            back = (C - shift) % C
            in_real = in_real + group_roll(g_real * w_real + g_imag * w_imag, back)
            in_imag = in_imag + group_roll(g_imag * w_real - g_real * w_imag, back)
        mixed = jnp.concatenate([unlines(in_real), unlines(in_imag)], axis=0)
        gout_ref[piece, own] = mixed.astype(BF16)
        gather_push(gout_ref.at[piece], sem(1, piece, 2))
        for shift in range(C):
            c_real = group_roll(real, shift)
            c_imag = group_roll(imaginary, shift)
            both = (c_real * g_real + c_imag * g_imag, c_real * g_imag - c_imag * g_real)
            for which in range(2):
                total = both[which][:half]
                for k in range(1, parts):
                    total = total + both[which][k * half : (k + 1) * half]
                if piece > 0:
                    total = total + total_ref[which, shift]
                total_ref[which, shift] = total

    def weight_terms():
        spot = lane_iota((half, LANES))
        lines = []
        for which in range(2):
            grads = [jnp.zeros((half, LANES), F32) for _ in range(C * C // LANES)]
            for shift in range(C):
                total = total_ref[which, shift]
                turn = C
                while turn < LANES:
                    total = total + pltpu.roll(total, turn, 1)
                    turn *= 2
                for k in range(C * C // LANES):
                    source = k * (LANES // C) + spot // C
                    match = (spot % C - source + C) % C == shift
                    grads[k] = jnp.where(match, total, grads[k])
            lines.append(jnp.concatenate(grads, axis=1))
        terms_ref[own] = jnp.concatenate(lines, axis=0).astype(BF16)
        gather_push(terms_ref, sem(2, 0, 0))

    for piece in range(HALVES):
        if_owner(functools.partial(mix_back, piece))
    if_owner(weight_terms)

    def finish(piece, index, carry):
        here = pl.ds(pl.multiple_of(index * chunk, chunk), chunk)
        part = strip(piece)
        spectral = dot(fwd_ref[here, :], gout_ref[piece].reshape(columns, wide))
        total = spectral.astype(BF16).astype(F32) + dot(pre_ref[here, part], mix_t_ref[...])
        grad_ref[here, part] = total.astype(BF16)
        return carry

    staged(1, gout_ref, finish)
    gather_pass(terms_ref, sem(2, 0, 0))
    end_sends(1, gout_ref)
    gather_wait(terms_ref, sem(2, 0, 0))
    gather_end(terms_ref, sem(2, 0, 0))

    def report(k, carry):
        terms = terms_ref[k].astype(F32)
        spec_ref[0, k] = terms[:half]
        spec_ref[1, k] = terms[half:]
        return carry

    lax.fori_loop(0, owners, report, 0)


def angle_tables(length, count, scale):
    frequencies = np.arange(count) - count // 2
    turns = np.arange(length)[:, None] * frequencies[None, :] % length
    angle = turns.astype(np.float32) * np.float32(2.0 * math.pi / length)
    return np.cos(angle) * np.float32(scale), np.sin(angle) * np.float32(scale)


def x_table(length):
    parts = []
    for scale in (1.0 / math.sqrt(length), 1.0 / math.sqrt(KX)):
        cosine, sine = angle_tables(length, KX, scale)
        parts += [cosine, -sine]
    table = np.concatenate(parts, axis=1)
    return np.pad(table, ((0, 0), (0, LANES - table.shape[1]))).astype(BF16)


def y_table(length):
    parts = []
    for scale in (1.0 / math.sqrt(length), 1.0 / math.sqrt(KY)):
        parts += list(angle_tables(length, KY, scale))
    table = np.concatenate(parts, axis=1)
    high = table.astype(BF16)
    low = (table - high.astype(np.float32)).astype(BF16)
    return np.concatenate([high, low], axis=1)


def shards(field, perm_class, perm_table, forcing, spec_weight, mix_weight, proj):
    gxn = lax.axis_size("gx")
    gyn = lax.axis_size("gy")
    n = gxn * gyn
    gx = lax.axis_index("gx")
    gy = lax.axis_index("gy")
    rows_x, rows_y, width = field.shape
    depth = width // C
    cells = rows_x * rows_y
    span_x = rows_x * gxn
    span_y = rows_y * gyn
    owners = min(n, KX * KY // 8)
    modes = KX * KY // owners
    block = 2 * modes
    columns = owners * block
    own = gx % 2 * (owners // 2) + (gx // 2 * gyn + gy) // (n // owners)
    weights = lax.dynamic_slice_in_dim(
        spec_weight.reshape(2, KX * KY, C, C), own * modes, modes, 1
    ).reshape(block, C * C)
    wide = width // HALVES
    step = wide

    vmem = pl.BlockSpec(memory_space=pltpu.VMEM)
    smem = pl.BlockSpec(memory_space=pltpu.SMEM)
    residual, grad_field, spec = pl.pallas_call(
        functools.partial(kernel, gxn, gyn, owners, rows_x, rows_y, depth),
        out_shape=(
            jax.ShapeDtypeStruct((rows_x, rows_y * depth), F32),
            jax.ShapeDtypeStruct((cells, width), BF16),
            jax.ShapeDtypeStruct((2, owners, modes, C * C), F32),
        ),
        in_specs=[vmem, vmem, smem] + [vmem] * 5 + [smem],
        out_specs=(vmem, vmem, vmem),
        scratch_shapes=[
            pltpu.VMEM((cells, columns), BF16),
            pltpu.VMEM((cells, columns), BF16),
            pltpu.VMEM((HALVES, owners, block, wide), BF16),
            pltpu.VMEM((2, HALVES, n // 2, block, wide), BF16),
            pltpu.VMEM((HALVES, owners, block, wide), BF16),
            pltpu.VMEM((HALVES, owners, block, wide), BF16),
            pltpu.VMEM((owners, block, C * C), BF16),
            pltpu.VMEM((2, C, modes, LANES), F32),
            pltpu.VMEM((cells, width), F32),
            pltpu.VMEM((cells, width), BF16),
            pltpu.VMEM((cells, LANES), F32),
            pltpu.VMEM((HALVES, 2, modes * wide // LANES, LANES), F32),
            pltpu.VMEM((2, HALVES, owners // 2, block, wide), BF16),
            pltpu.VMEM((HALVES, columns // 2, wide), F32),
            pltpu.VMEM((C, block, LANES), F32),
            pltpu.VMEM((step, step), BF16),
            pltpu.VMEM((step, step), BF16),
            pltpu.VMEM((1, width), F32),
            pltpu.VMEM((width, LANES), BF16),
            pltpu.VMEM((LANES, width), BF16),
            pltpu.VMEM((3, 2, 1, rows_y * depth), F32),
            pltpu.VMEM((3, 2, 1, rows_y * depth), F32),
            pltpu.VMEM((3, 2, rows_x, LANES), F32),
            pltpu.VMEM((3, 2, rows_x, LANES), F32),
            pltpu.SemaphoreType.DMA((18,)),
            pltpu.SemaphoreType.DMA((18,)),
            pltpu.SemaphoreType.DMA((3, 4)),
            pltpu.SemaphoreType.DMA((3, 4)),
        ],
        compiler_params=pltpu.CompilerParams(
            collective_id=0, has_side_effects=True, vmem_limit_bytes=60 * 1024 * 1024
        ),
        name="fourier_darcy",
    )(
        field.reshape(cells, width),
        perm_class,
        perm_table,
        forcing,
        jnp.asarray(x_table(span_x)),
        jnp.asarray(y_table(span_y)),
        weights,
        mix_weight,
        proj,
    )
    spec_grad = spec.reshape(2, KX, KY, C, C)
    return (residual, grad_field.reshape(rows_x, rows_y, width), spec_grad)


def solution(mesh):
    placed = (P("gx", "gy", None), P("gx", "gy"), P(), P("gx", "gy"), P(), P(), P())
    return jax.shard_map(
        shards,
        mesh=mesh,
        in_specs=placed,
        out_specs=(P("gx", "gy"), P("gx", "gy", None), P()),
        check_vma=False,
    )
```

```python
import functools
import math

import jax
import jax.numpy as jnp
import numpy as np
from jax import lax
from jax.experimental import pallas as pl
from jax.experimental.pallas import tpu as pltpu
from jax.sharding import PartitionSpec as P

C = 16
KX = 16
KY = 16
CLASSES = 8
LANES = 128
HALVES = 2
ROOT_HALF = 0.7071067811865476
INV_ROOT_TWO_PI = 0.3989422804014327
MESH = pl.DeviceIdType.MESH
F32 = jnp.float32
BF16 = jnp.bfloat16


def dot(left, right):
    return jnp.dot(left, right, preferred_element_type=F32)


def dot_first(left, right):
    return lax.dot_general(left, right, (((0,), (0,)), ((), ())), preferred_element_type=F32)


def split_dot(value, right):
    high = value.astype(BF16)
    low = (value - high.astype(F32)).astype(BF16)
    return dot(high, right) + dot(low, right)


def lane_iota(shape):
    return lax.broadcasted_iota(jnp.int32, shape, len(shape) - 1)


def group_roll(value, amount):
    if amount == 0:
        return value
    inside = lane_iota(value.shape) % C >= amount
    return jnp.where(
        inside, pltpu.roll(value, amount, 1), pltpu.roll(value, LANES - C + amount, 1)
    )


def kernel(
    gxn,
    gyn,
    owners,
    rows_x,
    rows_y,
    depth,
    field_in,
    class_ref,
    table_ref,
    forcing_ref,
    x_ref,
    y_ref,
    weight_ref,
    mixing_ref,
    proj_in,
    residual_ref,
    grad_ref,
    spec_ref,
    field_ref,
    bell_ref,
    applied_ref,
    load_sem,
    fwd_ref,
    inv_ref,
    send_ref,
    recv_ref,
    out_ref,
    gout_ref,
    terms_ref,
    total_ref,
    slope_ref,
    pre_ref,
    press_ref,
    coef_ref,
    pair_ref,
    half_ref,
    skew_ref,
    mix_ref,
    mix_t_ref,
    proj_ref,
    sum_ref,
    spread_ref,
    x_send,
    x_recv,
    y_send,
    y_recv,
    send_sem,
    recv_sem,
    halo_send,
    halo_recv,
):
    n = gxn * gyn
    gx = lax.axis_index("gx")
    gy = lax.axis_index("gy")
    core = gx % 2
    chips = n // 2
    chip = gx // 2 * gyn + gy
    apart = n // owners
    group = owners // 2
    own = core * group + chip // apart
    owner = chip % apart == 0
    cells = rows_x * rows_y
    width = depth * C
    block = 2 * KX * KY // owners
    half = block // 2
    per = LANES // depth
    span = rows_y * depth
    wide = width // HALVES
    parts = wide // LANES
    columns = owners * block

    def if_owner(body):
        if apart == 1:
            body()
        else:
            pl.when(owner)(body)

    def place(index):
        return (2 * (index // gyn) + core, index % gyn)

    load = pltpu.make_async_copy(field_in, field_ref, load_sem)
    load.start()
    sibling = (gx + 1 - 2 * core, gy)
    beside = gx - 1 + 2 * core
    has_beside = jnp.logical_and(beside >= 0, beside < gxn)
    barrier = pltpu.get_barrier_semaphore()

    def greet(k, carry):
        target = lax.rem(chip + k, chips)
        pl.semaphore_signal(barrier, inc=1, device_id=place(target), device_id_type=MESH)
        return carry

    lax.fori_loop(1, chips, greet, 0)
    pl.semaphore_signal(barrier, inc=1, device_id=sibling, device_id_type=MESH)

    @pl.when(has_beside)
    def _():
        pl.semaphore_signal(barrier, inc=1, device_id=(beside, gy), device_id_type=MESH)

    def chosen(shape, rule):
        row_at = lax.broadcasted_iota(jnp.int32, shape, 0)
        lane_at = lax.broadcasted_iota(jnp.int32, shape, 1)
        return rule(row_at, lane_at)

    def ones(shape, rule):
        return jnp.where(chosen(shape, rule), 1.0, 0.0).astype(BF16)

    def tables(which):
        shape = (LANES, columns)
        slot = lax.broadcasted_iota(jnp.int32, shape, 0)
        column = lax.broadcasted_iota(jnp.int32, shape, 1)
        mode = column // block * half + column % half
        first_mode = mode // KY + 2 * KX * which
        second_mode = mode % KY + 2 * KY * which
        imaginary = column % block >= half
        x_here = x_ref[pl.ds(pl.multiple_of(gx * rows_x, rows_x), rows_x), :]
        y_here = y_ref[pl.ds(pl.multiple_of(gy * rows_y, rows_y), rows_y), :]
        cosine = jnp.where(slot == first_mode, 1.0, 0.0)
        sine = jnp.where(slot == first_mode + KX, 1.0, 0.0)
        first = dot(x_here, jnp.where(imaginary, sine, cosine).astype(BF16))
        second = dot(x_here, jnp.where(imaginary, -cosine, sine).astype(BF16))
        fine = slot % (LANES // 2)
        y_cos = dot(y_here, jnp.where(fine == second_mode, 1.0, 0.0).astype(BF16))
        y_sin = dot(y_here, jnp.where(fine == second_mode + KY, 1.0, 0.0).astype(BF16))
        return first, second, y_cos, y_sin

    def fill(which, ref):
        first, second, y_cos, y_sin = tables(which)
        for x in range(rows_x):
            made = first[x : x + 1] * y_cos + second[x : x + 1] * y_sin
            ref[x * rows_y : (x + 1) * rows_y, :] = made.astype(BF16)

    fill(0, fwd_ref)
    pl.semaphore_wait(barrier, chips + jnp.where(has_beside, 1, 0))

    classes = class_ref[...]
    perm = jnp.zeros(classes.shape, F32)
    for level in range(CLASSES):
        perm = jnp.where(classes == level, table_ref[level], perm)

    sides = (
        (gx > 0, (gx - 1, gy), x_send, x_recv, 0),
        (gx < gxn - 1, (gx + 1, gy), x_send, x_recv, 1),
        (gy > 0, (gx, gy - 1), y_send, y_recv, 0),
        (gy < gyn - 1, (gx, gy + 1), y_send, y_recv, 1),
    )

    def halo_copy(turn, side):
        _, target, source, landing, end = sides[side]
        return pltpu.make_async_remote_copy(
            src_ref=source.at[turn, end],
            dst_ref=landing.at[turn, 1 - end],
            send_sem=halo_send.at[turn, side],
            recv_sem=halo_recv.at[turn, side ^ 1],
            device_id=target,
            device_id_type=MESH,
        )

    def halo_start(turn, value):
        x_send[turn, 0] = value[0:1, :]
        x_send[turn, 1] = value[rows_x - 1 : rows_x, :]
        y_send[turn, 0] = value[:, 0:LANES]
        y_send[turn, 1] = value[:, span - LANES : span]
        for side in range(4):
            there, _, _, landing, end = sides[side]

            @pl.when(there)
            def _():
                halo_copy(turn, side).start()

            @pl.when(jnp.logical_not(there))
            def _():
                landing[turn, end] = jnp.zeros(landing.shape[2:], F32)

    def halo_wait(turn):
        for side in range(4):
            there, _, _, landing, end = sides[side]

            @pl.when(there)
            def _():
                copy = halo_copy(turn, side)
                copy.wait_send()
                pltpu.make_async_copy(
                    landing.at[turn, end], landing.at[turn, end], halo_recv.at[turn, side]
                ).wait()

    row = lax.broadcasted_iota(jnp.int32, (rows_x, span), 0)
    layer = lane_iota((rows_x, span)) % depth
    column_at = lane_iota((rows_x, span))
    lane = lane_iota((rows_x, LANES))

    def neighbours(turn, value):
        below = jnp.where(row == 0, x_recv[turn, 0], pltpu.roll(value, 1, 0))
        above = jnp.where(row == rows_x - 1, x_recv[turn, 1], pltpu.roll(value, rows_x - 1, 0))
        moved = pltpu.roll(value, depth, 1)
        edge = jnp.where(lane < depth, pltpu.roll(y_recv[turn, 0], depth, 1), moved[:, :LANES])
        left = jnp.concatenate([edge, moved[:, LANES:]], axis=1)
        moved = pltpu.roll(value, span - depth, 1)
        edge = jnp.where(
            lane >= LANES - depth,
            pltpu.roll(y_recv[turn, 1], LANES - depth, 1),
            moved[:, span - LANES :],
        )
        right = jnp.concatenate([moved[:, : span - LANES], edge], axis=1)
        under = jnp.where(layer == 0, 0.0, pltpu.roll(value, 1, 1))
        over = jnp.where(layer == depth - 1, 0.0, pltpu.roll(value, span - 1, 1))
        return (below, above, left, right, under, over)

    halo_start(0, perm)

    def to_sibling(source, landing, sem):
        return pltpu.make_async_remote_copy(
            src_ref=source,
            dst_ref=landing,
            send_sem=send_sem.at[sem],
            recv_sem=recv_sem.at[sem],
            device_id=sibling,
            device_id_type=MESH,
        )

    def wait_chunks(ref, count, sem):
        held = ref.shape[0]
        for _ in range(count // held):
            pltpu.make_async_copy(ref, ref, sem).wait()
        if count % held:
            rest = ref.at[pl.ds(0, count % held)]
            pltpu.make_async_copy(rest, rest, sem).wait()

    def wait_owned(ref, sem):
        some = ref.at[pl.ds(0, group)]
        if_owner(lambda: wait_chunks(some, group - 1, sem))
        if apart > 1:
            pl.when(jnp.logical_not(owner))(lambda: wait_chunks(some, group, sem))

    mine = pl.ds(core * group, group)
    theirs = pl.ds((1 - core) * group, group)

    lanes = group * block

    def sem(phase, piece, stage):
        return (phase * HALVES + piece) * 4 + stage

    def strip(piece):
        return slice(piece * wide, (piece + 1) * wide)

    def product(which, piece, right_ref, table):
        start = pl.multiple_of(which * lanes, lanes)
        return dot_first(table[:, pl.ds(start, lanes)], right_ref[:, strip(piece)])

    def pair_copy(phase, piece):
        return to_sibling(
            send_ref.at[piece, theirs], pair_ref.at[phase, piece], sem(phase, piece, 0)
        )

    def give(phase, piece, right_ref, table):
        made = product(1 - core, piece, right_ref, table)
        send_ref[piece, theirs] = made.astype(BF16).reshape(group, block, wide)
        pair_copy(phase, piece).start()

    def keep(piece, right_ref, table):
        half_ref[piece] = product(core, piece, right_ref, table)

    def send(phase, piece):
        pair_copy(phase, piece).wait()
        total = half_ref[piece] + pair_ref[phase, piece].reshape(lanes, wide).astype(F32)
        send_ref[piece, mine] = total.astype(BF16).reshape(group, block, wide)

        def push(k, carry):
            target = k * apart

            @pl.when(target != chip)
            def _():
                pltpu.make_async_remote_copy(
                    src_ref=send_ref.at[piece, core * group + k],
                    dst_ref=recv_ref.at[phase, piece, chip],
                    send_sem=send_sem.at[sem(phase, piece, 1)],
                    recv_sem=recv_sem.at[sem(phase, piece, 1)],
                    device_id=place(target),
                    device_id_type=MESH,
                ).start()

            return carry

        lax.fori_loop(0, group, push, 0)

    def collect(phase, piece):
        recv_ref[phase, piece, chip] = send_ref[piece, own]
        wait_chunks(recv_ref.at[phase, piece], chips - 1, recv_sem.at[sem(phase, piece, 1)])

        def body(k, total):
            return total + recv_ref[phase, piece, k].astype(F32)

        total = lax.fori_loop(0, chips, body, jnp.zeros((block, wide), F32))

        def lines(part):
            return jnp.concatenate([part[:, k : k + LANES] for k in range(0, wide, LANES)], axis=0)

        return lines(total[:half]), lines(total[half:])

    def unlines(part):
        return jnp.concatenate([part[k * half : (k + 1) * half] for k in range(parts)], axis=1)

    def weights(shift):
        real = jnp.concatenate([skew_ref[shift, :half]] * parts, axis=0)
        imaginary = jnp.concatenate([skew_ref[shift, half:]] * parts, axis=0)
        return real, imaginary

    def gather_push(ref, at):
        def push(k, carry):
            target = lax.rem(chip + k, chips)
            pltpu.make_async_remote_copy(
                src_ref=ref.at[own],
                dst_ref=ref.at[own],
                send_sem=send_sem.at[at],
                recv_sem=recv_sem.at[at],
                device_id=place(target),
                device_id_type=MESH,
            ).start()
            return carry

        lax.fori_loop(1, chips, push, 0)

    def gather_pass(ref, at):
        wait_owned(ref, recv_sem.at[at])
        to_sibling(ref.at[mine], ref.at[mine], at + 1).start()

    def gather_wait(ref, at):
        to_sibling(ref.at[mine], ref.at[mine], at + 1).wait()

    def gather_end(ref, at):
        if_owner(lambda: wait_chunks(ref.at[pl.ds(0, group)], chips - 1, send_sem.at[at]))

    load.wait()
    give(0, 0, field_ref, fwd_ref)
    keep(0, field_ref, fwd_ref)
    give(0, 1, field_ref, fwd_ref)
    send(0, 0)
    keep(1, field_ref, fwd_ref)
    send(0, 1)

    fill(1, inv_ref)
    step = mix_ref.shape[0]
    repeat = ones((step, C), lambda r, l: r % C == l)
    repeat_t = ones((C, step), lambda r, l: r == l % C)
    blocks = chosen((step, step), lambda r, l: r // C == l // C)
    tall = dot(repeat, mixing_ref[...]).astype(BF16)
    mix_ref[...] = jnp.where(blocks, dot(tall, repeat_t), 0.0).astype(BF16)
    tall = lax.dot_general(
        repeat, mixing_ref[...], (((1,), (1,)), ((), ())), preferred_element_type=F32
    ).astype(BF16)
    mix_t_ref[...] = jnp.where(blocks, dot(tall, repeat_t), 0.0).astype(BF16)
    sum_ref[...] = ones(sum_ref.shape, lambda r, l: r // C == l % depth)
    spread_ref[...] = ones(spread_ref.shape, lambda r, l: l // C == r % depth)
    channel = lane_iota((1, width)) % C
    proj_row = jnp.zeros((1, width), F32)
    for k in range(C):
        proj_row = jnp.where(channel == k, proj_in[k], proj_row)
    proj_ref[...] = proj_row
    for shift in range(C):
        pick = ones(
            (C * C, LANES),
            lambda r, l: (r % C == l % C) & (r // C == (l % C - shift + C) % C),
        )
        skew_ref[shift] = dot(weight_ref[...], pick)

    def mix(piece):
        real, imaginary = collect(0, piece)
        coef_ref[piece, 0] = real
        coef_ref[piece, 1] = imaginary
        out_real = jnp.zeros_like(real)
        out_imag = jnp.zeros_like(real)
        for shift in range(C):
            w_real, w_imag = weights(shift)
            c_real = group_roll(real, shift)
            c_imag = group_roll(imaginary, shift)
            out_real = out_real + (c_real * w_real - c_imag * w_imag)
            out_imag = out_imag + (c_real * w_imag + c_imag * w_real)
        mixed = jnp.concatenate([unlines(out_real), unlines(out_imag)], axis=0)
        out_ref[piece, own] = mixed.astype(BF16)
        gather_push(out_ref.at[piece], sem(0, piece, 2))

    for piece in range(HALVES):
        if_owner(functools.partial(mix, piece))

    chunk = 4 * rows_y
    steps = cells // chunk

    def activate(piece, index, carry):
        here = pl.ds(pl.multiple_of(index * chunk, chunk), chunk)
        part = strip(piece)
        spectral = dot(inv_ref[here, :], out_ref[piece].reshape(columns, wide))
        preact = spectral.astype(BF16).astype(F32) + dot(field_ref[here, part], mix_ref[...])
        bell = 0.5 * (1.0 + lax.erf(preact * ROOT_HALF))
        row_proj = proj_ref[:, part]
        slope_ref[here, part] = preact
        bell_ref[here, part] = bell
        share = split_dot(preact * bell * row_proj, sum_ref[part, :])
        press_ref[here, :] = share if piece == 0 else press_ref[here, :] + share
        return carry

    def staged(phase, ref, work):
        gather_pass(ref.at[0], sem(phase, 0, 2))
        gather_wait(ref.at[0], sem(phase, 0, 2))
        lax.fori_loop(0, steps // 2, functools.partial(work, 0), 0)
        gather_pass(ref.at[1], sem(phase, 1, 2))
        lax.fori_loop(steps // 2, steps, functools.partial(work, 0), 0)
        gather_wait(ref.at[1], sem(phase, 1, 2))
        lax.fori_loop(0, steps, functools.partial(work, 1), 0)

    def end_sends(phase, ref):
        for piece in range(HALVES):
            gather_end(ref.at[piece], sem(phase, piece, 2))
            wait_owned(send_ref.at[piece], send_sem.at[sem(phase, piece, 1)])

    staged(0, out_ref, activate)

    def gathered(index):
        made = press_ref[pl.ds(index * per, rows_x, stride=rows_y), :]
        for k in range(1, per):
            other = press_ref[pl.ds(index * per + k, rows_x, stride=rows_y), :]
            made = jnp.where(lane // depth == k, other, made)
        return made

    end_sends(0, out_ref)
    pressure = jnp.concatenate([gathered(k) for k in range(rows_y // per)], axis=1)
    halo_start(1, pressure)

    def slope(piece, index, carry):
        here = pl.ds(pl.multiple_of(index * chunk, chunk), chunk)
        part = strip(piece)
        preact = slope_ref[here, part]
        tail = preact * jnp.exp(-0.5 * preact * preact) * INV_ROOT_TWO_PI
        slope_ref[here, part] = (bell_ref[here, part] + tail) * proj_ref[:, part]
        return carry

    halo_wait(0)
    means = [0.5 * (perm + other) for other in neighbours(0, perm)]

    def operator_inside(value):
        def term(mean, axis, amount, outside):
            made = mean * (value - pltpu.roll(value, amount, axis))
            return jnp.where(outside, 0.0, made)

        total = means[4] * (value - jnp.where(layer == 0, 0.0, pltpu.roll(value, 1, 1)))
        total = total + means[5] * (
            value - jnp.where(layer == depth - 1, 0.0, pltpu.roll(value, span - 1, 1))
        )
        total = total + term(means[0], 0, 1, row == 0)
        total = total + term(means[1], 0, rows_x - 1, row == rows_x - 1)
        total = total + term(means[2], 1, depth, column_at < depth)
        return total + term(means[3], 1, span - depth, column_at >= span - depth)

    def operator_faces(turn, value, ref):
        last = rows_x - 1
        ref[0:1, :] += means[0][0:1] * (value[0:1] - x_recv[turn, 0])
        ref[last : last + 1, :] += means[1][last:] * (value[last:] - x_recv[turn, 1])
        other = pltpu.roll(y_recv[turn, 0], depth, 1)
        made = means[2][:, :LANES] * (value[:, :LANES] - other)
        ref[:, :LANES] += jnp.where(lane < depth, made, 0.0)
        other = pltpu.roll(y_recv[turn, 1], LANES - depth, 1)
        made = means[3][:, span - LANES :] * (value[:, span - LANES :] - other)
        ref[:, span - LANES :] += jnp.where(lane >= LANES - depth, made, 0.0)

    residual_ref[...] = operator_inside(pressure) - forcing_ref[...]
    lax.fori_loop(0, steps, functools.partial(slope, 0), 0)
    halo_wait(1)
    operator_faces(1, pressure, residual_ref)
    residual = residual_ref[...]
    halo_start(2, residual)
    applied_ref[...] = operator_inside(residual)
    lax.fori_loop(0, steps, functools.partial(slope, 1), 0)
    halo_wait(2)
    operator_faces(2, residual, applied_ref)
    slope_source = applied_ref[...]
    for k in range(rows_y // per):
        piece = slope_source[:, k * LANES : (k + 1) * LANES]
        for j in range(per):
            press_ref[pl.ds(k * per + j, rows_x, stride=rows_y), :] = jnp.where(
                lane // depth == j, piece, 0.0
            )

    def differentiate(piece, index, carry):
        here = pl.ds(pl.multiple_of(index * chunk, chunk), chunk)
        part = strip(piece)
        source = split_dot(press_ref[here, :], spread_ref[:, part])
        pre_ref[here, part] = (source * slope_ref[here, part]).astype(BF16)
        return carry

    lax.fori_loop(0, steps, functools.partial(differentiate, 0), 0)
    give(1, 0, pre_ref, inv_ref)
    keep(0, pre_ref, inv_ref)
    lax.fori_loop(0, steps, functools.partial(differentiate, 1), 0)
    send(1, 0)
    give(1, 1, pre_ref, inv_ref)
    keep(1, pre_ref, inv_ref)
    send(1, 1)

    def mix_back(piece):
        g_real, g_imag = collect(1, piece)
        real = coef_ref[piece, 0]
        imaginary = coef_ref[piece, 1]
        in_real = jnp.zeros_like(real)
        in_imag = jnp.zeros_like(real)
        for shift in range(C):
            w_real, w_imag = weights(shift)
            back = (C - shift) % C
            in_real = in_real + group_roll(g_real * w_real + g_imag * w_imag, back)
            in_imag = in_imag + group_roll(g_imag * w_real - g_real * w_imag, back)
        mixed = jnp.concatenate([unlines(in_real), unlines(in_imag)], axis=0)
        gout_ref[piece, own] = mixed.astype(BF16)
        gather_push(gout_ref.at[piece], sem(1, piece, 2))
        for shift in range(C):
            c_real = group_roll(real, shift)
            c_imag = group_roll(imaginary, shift)
            both = (c_real * g_real + c_imag * g_imag, c_real * g_imag - c_imag * g_real)
            for which in range(2):
                total = both[which][:half]
                for k in range(1, parts):
                    total = total + both[which][k * half : (k + 1) * half]
                if piece > 0:
                    total = total + total_ref[which, shift]
                total_ref[which, shift] = total

    def weight_terms():
        spot = lane_iota((half, LANES))
        lines = []
        for which in range(2):
            grads = [jnp.zeros((half, LANES), F32) for _ in range(C * C // LANES)]
            for shift in range(C):
                total = total_ref[which, shift]
                turn = C
                while turn < LANES:
                    total = total + pltpu.roll(total, turn, 1)
                    turn *= 2
                for k in range(C * C // LANES):
                    source = k * (LANES // C) + spot // C
                    match = (spot % C - source + C) % C == shift
                    grads[k] = jnp.where(match, total, grads[k])
            lines.append(jnp.concatenate(grads, axis=1))
        terms_ref[own] = jnp.concatenate(lines, axis=0).astype(BF16)
        gather_push(terms_ref, sem(2, 0, 0))

    for piece in range(HALVES):
        if_owner(functools.partial(mix_back, piece))
    if_owner(weight_terms)

    def finish(piece, index, carry):
        here = pl.ds(pl.multiple_of(index * chunk, chunk), chunk)
        part = strip(piece)
        spectral = dot(fwd_ref[here, :], gout_ref[piece].reshape(columns, wide))
        total = spectral.astype(BF16).astype(F32) + dot(pre_ref[here, part], mix_t_ref[...])
        grad_ref[here, part] = total.astype(BF16)
        return carry

    staged(1, gout_ref, finish)
    gather_pass(terms_ref, sem(2, 0, 0))
    end_sends(1, gout_ref)
    gather_wait(terms_ref, sem(2, 0, 0))
    gather_end(terms_ref, sem(2, 0, 0))

    def report(k, carry):
        terms = terms_ref[k].astype(F32)
        spec_ref[0, k] = terms[:half]
        spec_ref[1, k] = terms[half:]
        return carry

    lax.fori_loop(0, owners, report, 0)


def angle_tables(length, count, scale):
    frequencies = np.arange(count) - count // 2
    turns = np.arange(length)[:, None] * frequencies[None, :] % length
    angle = turns.astype(np.float32) * np.float32(2.0 * math.pi / length)
    return np.cos(angle) * np.float32(scale), np.sin(angle) * np.float32(scale)


def x_table(length):
    parts = []
    for scale in (1.0 / math.sqrt(length), 1.0 / math.sqrt(KX)):
        cosine, sine = angle_tables(length, KX, scale)
        parts += [cosine, -sine]
    table = np.concatenate(parts, axis=1)
    return np.pad(table, ((0, 0), (0, LANES - table.shape[1]))).astype(BF16)


def y_table(length):
    parts = []
    for scale in (1.0 / math.sqrt(length), 1.0 / math.sqrt(KY)):
        parts += list(angle_tables(length, KY, scale))
    table = np.concatenate(parts, axis=1)
    high = table.astype(BF16)
    low = (table - high.astype(np.float32)).astype(BF16)
    return np.concatenate([high, low], axis=1)


def shards(field, perm_class, perm_table, forcing, spec_weight, mix_weight, proj):
    gxn = lax.axis_size("gx")
    gyn = lax.axis_size("gy")
    n = gxn * gyn
    gx = lax.axis_index("gx")
    gy = lax.axis_index("gy")
    rows_x, rows_y, width = field.shape
    depth = width // C
    cells = rows_x * rows_y
    span_x = rows_x * gxn
    span_y = rows_y * gyn
    owners = min(n, KX * KY // 8)
    modes = KX * KY // owners
    block = 2 * modes
    columns = owners * block
    own = gx % 2 * (owners // 2) + (gx // 2 * gyn + gy) // (n // owners)
    weights = lax.dynamic_slice_in_dim(
        spec_weight.reshape(2, KX * KY, C, C), own * modes, modes, 1
    ).reshape(block, C * C)
    wide = width // HALVES
    step = wide

    vmem = pl.BlockSpec(memory_space=pltpu.VMEM)
    smem = pl.BlockSpec(memory_space=pltpu.SMEM)
    residual, grad_field, spec = pl.pallas_call(
        functools.partial(kernel, gxn, gyn, owners, rows_x, rows_y, depth),
        out_shape=(
            jax.ShapeDtypeStruct((rows_x, rows_y * depth), F32),
            jax.ShapeDtypeStruct((cells, width), BF16),
            jax.ShapeDtypeStruct((2, owners, modes, C * C), F32),
        ),
        in_specs=[pl.BlockSpec(memory_space=pl.ANY), vmem, smem] + [vmem] * 5 + [smem],
        out_specs=(vmem, vmem, vmem),
        scratch_shapes=[
            pltpu.VMEM((cells, width), BF16),
            pltpu.VMEM((cells, width), F32),
            pltpu.VMEM((rows_x, rows_y * depth), F32),
            pltpu.SemaphoreType.DMA,
            pltpu.VMEM((cells, columns), BF16),
            pltpu.VMEM((cells, columns), BF16),
            pltpu.VMEM((HALVES, owners, block, wide), BF16),
            pltpu.VMEM((2, HALVES, n // 2, block, wide), BF16),
            pltpu.VMEM((HALVES, owners, block, wide), BF16),
            pltpu.VMEM((HALVES, owners, block, wide), BF16),
            pltpu.VMEM((owners, block, C * C), BF16),
            pltpu.VMEM((2, C, modes, LANES), F32),
            pltpu.VMEM((cells, width), F32),
            pltpu.VMEM((cells, width), BF16),
            pltpu.VMEM((cells, LANES), F32),
            pltpu.VMEM((HALVES, 2, modes * wide // LANES, LANES), F32),
            pltpu.VMEM((2, HALVES, owners // 2, block, wide), BF16),
            pltpu.VMEM((HALVES, columns // 2, wide), F32),
            pltpu.VMEM((C, block, LANES), F32),
            pltpu.VMEM((step, step), BF16),
            pltpu.VMEM((step, step), BF16),
            pltpu.VMEM((1, width), F32),
            pltpu.VMEM((width, LANES), BF16),
            pltpu.VMEM((LANES, width), BF16),
            pltpu.VMEM((3, 2, 1, rows_y * depth), F32),
            pltpu.VMEM((3, 2, 1, rows_y * depth), F32),
            pltpu.VMEM((3, 2, rows_x, LANES), F32),
            pltpu.VMEM((3, 2, rows_x, LANES), F32),
            pltpu.SemaphoreType.DMA((18,)),
            pltpu.SemaphoreType.DMA((18,)),
            pltpu.SemaphoreType.DMA((3, 4)),
            pltpu.SemaphoreType.DMA((3, 4)),
        ],
        compiler_params=pltpu.CompilerParams(
            collective_id=0, has_side_effects=True, vmem_limit_bytes=60 * 1024 * 1024
        ),
        name="fourier_darcy",
    )(
        field.reshape(cells, width),
        perm_class,
        perm_table,
        forcing,
        jnp.asarray(x_table(span_x)),
        jnp.asarray(y_table(span_y)),
        weights,
        mix_weight,
        proj,
    )
    spec_grad = spec.reshape(2, KX, KY, C, C)
    return (residual, grad_field.reshape(rows_x, rows_y, width), spec_grad)


def solution(mesh):
    placed = (P("gx", "gy", None), P("gx", "gy"), P(), P("gx", "gy"), P(), P(), P())
    return jax.shard_map(
        shards,
        mesh=mesh,
        in_specs=placed,
        out_specs=(P("gx", "gy"), P("gx", "gy", None), P()),
        check_vma=False,
    )
```

```python
import functools
import math

import jax
import jax.numpy as jnp
import numpy as np
from jax import lax
from jax.experimental import pallas as pl
from jax.experimental.pallas import tpu as pltpu
from jax.sharding import PartitionSpec as P

C = 16
KX = 16
KY = 16
CLASSES = 8
LANES = 128
HALVES = 2
ROOT_HALF = 0.7071067811865476
INV_ROOT_TWO_PI = 0.3989422804014327
MESH = pl.DeviceIdType.MESH
F32 = jnp.float32
BF16 = jnp.bfloat16


def dot(left, right):
    return jnp.dot(left, right, preferred_element_type=F32)


def dot_first(left, right):
    return lax.dot_general(left, right, (((0,), (0,)), ((), ())), preferred_element_type=F32)


def split_dot(value, right):
    high = value.astype(BF16)
    low = (value - high.astype(F32)).astype(BF16)
    return dot(high, right) + dot(low, right)


def lane_iota(shape):
    return lax.broadcasted_iota(jnp.int32, shape, len(shape) - 1)


def group_roll(value, amount):
    if amount == 0:
        return value
    inside = lane_iota(value.shape) % C >= amount
    return jnp.where(
        inside, pltpu.roll(value, amount, 1), pltpu.roll(value, LANES - C + amount, 1)
    )


def kernel(
    gxn,
    gyn,
    owners,
    rows_x,
    rows_y,
    depth,
    field_in,
    class_ref,
    table_ref,
    forcing_ref,
    x_ref,
    y_ref,
    weight_ref,
    mixing_ref,
    proj_in,
    residual_ref,
    grad_out,
    spec_ref,
    grad_ref,
    store_sem,
    field_ref,
    bell_ref,
    applied_ref,
    load_sem,
    fwd_ref,
    inv_ref,
    send_ref,
    recv_ref,
    out_ref,
    gout_ref,
    terms_ref,
    total_ref,
    slope_ref,
    pre_ref,
    press_ref,
    coef_ref,
    pair_ref,
    half_ref,
    skew_ref,
    mix_ref,
    mix_t_ref,
    proj_ref,
    sum_ref,
    spread_ref,
    x_send,
    x_recv,
    y_send,
    y_recv,
    send_sem,
    recv_sem,
    halo_send,
    halo_recv,
):
    n = gxn * gyn
    gx = lax.axis_index("gx")
    gy = lax.axis_index("gy")
    core = gx % 2
    chips = n // 2
    chip = gx // 2 * gyn + gy
    apart = n // owners
    group = owners // 2
    own = core * group + chip // apart
    owner = chip % apart == 0
    cells = rows_x * rows_y
    width = depth * C
    block = 2 * KX * KY // owners
    half = block // 2
    per = LANES // depth
    span = rows_y * depth
    wide = width // HALVES
    parts = wide // LANES
    columns = owners * block

    def if_owner(body):
        if apart == 1:
            body()
        else:
            pl.when(owner)(body)

    def place(index):
        return (2 * (index // gyn) + core, index % gyn)

    load = pltpu.make_async_copy(field_in, field_ref, load_sem)
    load.start()
    sibling = (gx + 1 - 2 * core, gy)
    beside = gx - 1 + 2 * core
    has_beside = jnp.logical_and(beside >= 0, beside < gxn)
    barrier = pltpu.get_barrier_semaphore()

    def greet(k, carry):
        target = lax.rem(chip + k, chips)
        pl.semaphore_signal(barrier, inc=1, device_id=place(target), device_id_type=MESH)
        return carry

    lax.fori_loop(1, chips, greet, 0)
    pl.semaphore_signal(barrier, inc=1, device_id=sibling, device_id_type=MESH)

    @pl.when(has_beside)
    def _():
        pl.semaphore_signal(barrier, inc=1, device_id=(beside, gy), device_id_type=MESH)

    def chosen(shape, rule):
        row_at = lax.broadcasted_iota(jnp.int32, shape, 0)
        lane_at = lax.broadcasted_iota(jnp.int32, shape, 1)
        return rule(row_at, lane_at)

    def ones(shape, rule):
        return jnp.where(chosen(shape, rule), 1.0, 0.0).astype(BF16)

    def tables(which):
        shape = (LANES, columns)
        slot = lax.broadcasted_iota(jnp.int32, shape, 0)
        column = lax.broadcasted_iota(jnp.int32, shape, 1)
        mode = column // block * half + column % half
        first_mode = mode // KY + 2 * KX * which
        second_mode = mode % KY + 2 * KY * which
        imaginary = column % block >= half
        x_here = x_ref[pl.ds(pl.multiple_of(gx * rows_x, rows_x), rows_x), :]
        y_here = y_ref[pl.ds(pl.multiple_of(gy * rows_y, rows_y), rows_y), :]
        cosine = jnp.where(slot == first_mode, 1.0, 0.0)
        sine = jnp.where(slot == first_mode + KX, 1.0, 0.0)
        first = dot(x_here, jnp.where(imaginary, sine, cosine).astype(BF16))
        second = dot(x_here, jnp.where(imaginary, -cosine, sine).astype(BF16))
        fine = slot % (LANES // 2)
        y_cos = dot(y_here, jnp.where(fine == second_mode, 1.0, 0.0).astype(BF16))
        y_sin = dot(y_here, jnp.where(fine == second_mode + KY, 1.0, 0.0).astype(BF16))
        return first, second, y_cos, y_sin

    def fill(which, ref):
        first, second, y_cos, y_sin = tables(which)
        for x in range(rows_x):
            made = first[x : x + 1] * y_cos + second[x : x + 1] * y_sin
            ref[x * rows_y : (x + 1) * rows_y, :] = made.astype(BF16)

    fill(0, fwd_ref)
    pl.semaphore_wait(barrier, chips + jnp.where(has_beside, 1, 0))

    classes = class_ref[...]
    perm = jnp.zeros(classes.shape, F32)
    for level in range(CLASSES):
        perm = jnp.where(classes == level, table_ref[level], perm)

    sides = (
        (gx > 0, (gx - 1, gy), x_send, x_recv, 0),
        (gx < gxn - 1, (gx + 1, gy), x_send, x_recv, 1),
        (gy > 0, (gx, gy - 1), y_send, y_recv, 0),
        (gy < gyn - 1, (gx, gy + 1), y_send, y_recv, 1),
    )

    def halo_copy(turn, side):
        _, target, source, landing, end = sides[side]
        return pltpu.make_async_remote_copy(
            src_ref=source.at[turn, end],
            dst_ref=landing.at[turn, 1 - end],
            send_sem=halo_send.at[turn, side],
            recv_sem=halo_recv.at[turn, side ^ 1],
            device_id=target,
            device_id_type=MESH,
        )

    def halo_start(turn, value):
        x_send[turn, 0] = value[0:1, :]
        x_send[turn, 1] = value[rows_x - 1 : rows_x, :]
        y_send[turn, 0] = value[:, 0:LANES]
        y_send[turn, 1] = value[:, span - LANES : span]
        for side in range(4):
            there, _, _, landing, end = sides[side]

            @pl.when(there)
            def _():
                halo_copy(turn, side).start()

            @pl.when(jnp.logical_not(there))
            def _():
                landing[turn, end] = jnp.zeros(landing.shape[2:], F32)

    def halo_wait(turn):
        for side in range(4):
            there, _, _, landing, end = sides[side]

            @pl.when(there)
            def _():
                copy = halo_copy(turn, side)
                copy.wait_send()
                pltpu.make_async_copy(
                    landing.at[turn, end], landing.at[turn, end], halo_recv.at[turn, side]
                ).wait()

    row = lax.broadcasted_iota(jnp.int32, (rows_x, span), 0)
    layer = lane_iota((rows_x, span)) % depth
    column_at = lane_iota((rows_x, span))
    lane = lane_iota((rows_x, LANES))

    def neighbours(turn, value):
        below = jnp.where(row == 0, x_recv[turn, 0], pltpu.roll(value, 1, 0))
        above = jnp.where(row == rows_x - 1, x_recv[turn, 1], pltpu.roll(value, rows_x - 1, 0))
        moved = pltpu.roll(value, depth, 1)
        edge = jnp.where(lane < depth, pltpu.roll(y_recv[turn, 0], depth, 1), moved[:, :LANES])
        left = jnp.concatenate([edge, moved[:, LANES:]], axis=1)
        moved = pltpu.roll(value, span - depth, 1)
        edge = jnp.where(
            lane >= LANES - depth,
            pltpu.roll(y_recv[turn, 1], LANES - depth, 1),
            moved[:, span - LANES :],
        )
        right = jnp.concatenate([moved[:, : span - LANES], edge], axis=1)
        under = jnp.where(layer == 0, 0.0, pltpu.roll(value, 1, 1))
        over = jnp.where(layer == depth - 1, 0.0, pltpu.roll(value, span - 1, 1))
        return (below, above, left, right, under, over)

    halo_start(0, perm)

    def to_sibling(source, landing, sem):
        return pltpu.make_async_remote_copy(
            src_ref=source,
            dst_ref=landing,
            send_sem=send_sem.at[sem],
            recv_sem=recv_sem.at[sem],
            device_id=sibling,
            device_id_type=MESH,
        )

    def wait_chunks(ref, count, sem):
        held = ref.shape[0]
        for _ in range(count // held):
            pltpu.make_async_copy(ref, ref, sem).wait()
        if count % held:
            rest = ref.at[pl.ds(0, count % held)]
            pltpu.make_async_copy(rest, rest, sem).wait()

    def wait_owned(ref, sem):
        some = ref.at[pl.ds(0, group)]
        if_owner(lambda: wait_chunks(some, group - 1, sem))
        if apart > 1:
            pl.when(jnp.logical_not(owner))(lambda: wait_chunks(some, group, sem))

    mine = pl.ds(core * group, group)
    theirs = pl.ds((1 - core) * group, group)

    lanes = group * block

    def sem(phase, piece, stage):
        return (phase * HALVES + piece) * 4 + stage

    def strip(piece):
        return slice(piece * wide, (piece + 1) * wide)

    def product(which, piece, right_ref, table):
        start = pl.multiple_of(which * lanes, lanes)
        return dot_first(table[:, pl.ds(start, lanes)], right_ref[:, strip(piece)])

    def pair_copy(phase, piece):
        return to_sibling(
            send_ref.at[piece, theirs], pair_ref.at[phase, piece], sem(phase, piece, 0)
        )

    def give(phase, piece, right_ref, table):
        made = product(1 - core, piece, right_ref, table)
        send_ref[piece, theirs] = made.astype(BF16).reshape(group, block, wide)
        pair_copy(phase, piece).start()

    def keep(piece, right_ref, table):
        half_ref[piece] = product(core, piece, right_ref, table)

    def send(phase, piece):
        pair_copy(phase, piece).wait()
        total = half_ref[piece] + pair_ref[phase, piece].reshape(lanes, wide).astype(F32)
        send_ref[piece, mine] = total.astype(BF16).reshape(group, block, wide)

        def push(k, carry):
            target = k * apart

            @pl.when(target != chip)
            def _():
                pltpu.make_async_remote_copy(
                    src_ref=send_ref.at[piece, core * group + k],
                    dst_ref=recv_ref.at[phase, piece, chip],
                    send_sem=send_sem.at[sem(phase, piece, 1)],
                    recv_sem=recv_sem.at[sem(phase, piece, 1)],
                    device_id=place(target),
                    device_id_type=MESH,
                ).start()

            return carry

        lax.fori_loop(0, group, push, 0)

    def collect(phase, piece):
        recv_ref[phase, piece, chip] = send_ref[piece, own]
        wait_chunks(recv_ref.at[phase, piece], chips - 1, recv_sem.at[sem(phase, piece, 1)])

        def body(k, total):
            return total + recv_ref[phase, piece, k].astype(F32)

        total = lax.fori_loop(0, chips, body, jnp.zeros((block, wide), F32))

        def lines(part):
            return jnp.concatenate([part[:, k : k + LANES] for k in range(0, wide, LANES)], axis=0)

        return lines(total[:half]), lines(total[half:])

    def unlines(part):
        return jnp.concatenate([part[k * half : (k + 1) * half] for k in range(parts)], axis=1)

    def weights(shift):
        real = jnp.concatenate([skew_ref[shift, :half]] * parts, axis=0)
        imaginary = jnp.concatenate([skew_ref[shift, half:]] * parts, axis=0)
        return real, imaginary

    def gather_push(ref, at):
        def push(k, carry):
            target = lax.rem(chip + k, chips)
            pltpu.make_async_remote_copy(
                src_ref=ref.at[own],
                dst_ref=ref.at[own],
                send_sem=send_sem.at[at],
                recv_sem=recv_sem.at[at],
                device_id=place(target),
                device_id_type=MESH,
            ).start()
            return carry

        lax.fori_loop(1, chips, push, 0)

    def gather_pass(ref, at):
        wait_owned(ref, recv_sem.at[at])
        to_sibling(ref.at[mine], ref.at[mine], at + 1).start()

    def gather_wait(ref, at):
        to_sibling(ref.at[mine], ref.at[mine], at + 1).wait()

    def gather_end(ref, at):
        if_owner(lambda: wait_chunks(ref.at[pl.ds(0, group)], chips - 1, send_sem.at[at]))

    load.wait()
    give(0, 0, field_ref, fwd_ref)
    keep(0, field_ref, fwd_ref)
    give(0, 1, field_ref, fwd_ref)
    send(0, 0)
    keep(1, field_ref, fwd_ref)
    send(0, 1)

    fill(1, inv_ref)
    step = mix_ref.shape[0]
    repeat = ones((step, C), lambda r, l: r % C == l)
    repeat_t = ones((C, step), lambda r, l: r == l % C)
    blocks = chosen((step, step), lambda r, l: r // C == l // C)
    tall = dot(repeat, mixing_ref[...]).astype(BF16)
    mix_ref[...] = jnp.where(blocks, dot(tall, repeat_t), 0.0).astype(BF16)
    tall = lax.dot_general(
        repeat, mixing_ref[...], (((1,), (1,)), ((), ())), preferred_element_type=F32
    ).astype(BF16)
    mix_t_ref[...] = jnp.where(blocks, dot(tall, repeat_t), 0.0).astype(BF16)
    sum_ref[...] = ones(sum_ref.shape, lambda r, l: r // C == l % depth)
    spread_ref[...] = ones(spread_ref.shape, lambda r, l: l // C == r % depth)
    channel = lane_iota((1, width)) % C
    proj_row = jnp.zeros((1, width), F32)
    for k in range(C):
        proj_row = jnp.where(channel == k, proj_in[k], proj_row)
    proj_ref[...] = proj_row
    for shift in range(C):
        pick = ones(
            (C * C, LANES),
            lambda r, l: (r % C == l % C) & (r // C == (l % C - shift + C) % C),
        )
        skew_ref[shift] = dot(weight_ref[...], pick)

    def mix(piece):
        real, imaginary = collect(0, piece)
        coef_ref[piece, 0] = real
        coef_ref[piece, 1] = imaginary
        out_real = jnp.zeros_like(real)
        out_imag = jnp.zeros_like(real)
        for shift in range(C):
            w_real, w_imag = weights(shift)
            c_real = group_roll(real, shift)
            c_imag = group_roll(imaginary, shift)
            out_real = out_real + (c_real * w_real - c_imag * w_imag)
            out_imag = out_imag + (c_real * w_imag + c_imag * w_real)
        mixed = jnp.concatenate([unlines(out_real), unlines(out_imag)], axis=0)
        out_ref[piece, own] = mixed.astype(BF16)
        gather_push(out_ref.at[piece], sem(0, piece, 2))

    for piece in range(HALVES):
        if_owner(functools.partial(mix, piece))

    chunk = 4 * rows_y
    steps = cells // chunk

    def activate(piece, index, carry):
        here = pl.ds(pl.multiple_of(index * chunk, chunk), chunk)
        part = strip(piece)
        spectral = dot(inv_ref[here, :], out_ref[piece].reshape(columns, wide))
        preact = spectral.astype(BF16).astype(F32) + dot(field_ref[here, part], mix_ref[...])
        bell = 0.5 * (1.0 + lax.erf(preact * ROOT_HALF))
        row_proj = proj_ref[:, part]
        slope_ref[here, part] = preact
        bell_ref[here, part] = bell
        share = split_dot(preact * bell * row_proj, sum_ref[part, :])
        press_ref[here, :] = share if piece == 0 else press_ref[here, :] + share
        return carry

    def staged(phase, ref, work):
        gather_pass(ref.at[0], sem(phase, 0, 2))
        gather_wait(ref.at[0], sem(phase, 0, 2))
        lax.fori_loop(0, steps // 2, functools.partial(work, 0), 0)
        gather_pass(ref.at[1], sem(phase, 1, 2))
        lax.fori_loop(steps // 2, steps, functools.partial(work, 0), 0)
        gather_wait(ref.at[1], sem(phase, 1, 2))
        lax.fori_loop(0, steps, functools.partial(work, 1), 0)

    def end_sends(phase, ref):
        for piece in range(HALVES):
            gather_end(ref.at[piece], sem(phase, piece, 2))
            wait_owned(send_ref.at[piece], send_sem.at[sem(phase, piece, 1)])

    staged(0, out_ref, activate)

    def gathered(index):
        made = press_ref[pl.ds(index * per, rows_x, stride=rows_y), :]
        for k in range(1, per):
            other = press_ref[pl.ds(index * per + k, rows_x, stride=rows_y), :]
            made = jnp.where(lane // depth == k, other, made)
        return made

    end_sends(0, out_ref)
    pressure = jnp.concatenate([gathered(k) for k in range(rows_y // per)], axis=1)
    halo_start(1, pressure)

    def slope(piece, index, carry):
        here = pl.ds(pl.multiple_of(index * chunk, chunk), chunk)
        part = strip(piece)
        preact = slope_ref[here, part]
        tail = preact * jnp.exp(-0.5 * preact * preact) * INV_ROOT_TWO_PI
        slope_ref[here, part] = (bell_ref[here, part] + tail) * proj_ref[:, part]
        return carry

    halo_wait(0)
    means = [0.5 * (perm + other) for other in neighbours(0, perm)]

    def operator_inside(value):
        def term(mean, axis, amount, outside):
            made = mean * (value - pltpu.roll(value, amount, axis))
            return jnp.where(outside, 0.0, made)

        total = means[4] * (value - jnp.where(layer == 0, 0.0, pltpu.roll(value, 1, 1)))
        total = total + means[5] * (
            value - jnp.where(layer == depth - 1, 0.0, pltpu.roll(value, span - 1, 1))
        )
        total = total + term(means[0], 0, 1, row == 0)
        total = total + term(means[1], 0, rows_x - 1, row == rows_x - 1)
        total = total + term(means[2], 1, depth, column_at < depth)
        return total + term(means[3], 1, span - depth, column_at >= span - depth)

    def operator_faces(turn, value, ref):
        last = rows_x - 1
        ref[0:1, :] += means[0][0:1] * (value[0:1] - x_recv[turn, 0])
        ref[last : last + 1, :] += means[1][last:] * (value[last:] - x_recv[turn, 1])
        other = pltpu.roll(y_recv[turn, 0], depth, 1)
        made = means[2][:, :LANES] * (value[:, :LANES] - other)
        ref[:, :LANES] += jnp.where(lane < depth, made, 0.0)
        other = pltpu.roll(y_recv[turn, 1], LANES - depth, 1)
        made = means[3][:, span - LANES :] * (value[:, span - LANES :] - other)
        ref[:, span - LANES :] += jnp.where(lane >= LANES - depth, made, 0.0)

    residual_ref[...] = operator_inside(pressure) - forcing_ref[...]
    lax.fori_loop(0, steps, functools.partial(slope, 0), 0)
    halo_wait(1)
    operator_faces(1, pressure, residual_ref)
    residual = residual_ref[...]
    halo_start(2, residual)
    applied_ref[...] = operator_inside(residual)
    lax.fori_loop(0, steps, functools.partial(slope, 1), 0)
    halo_wait(2)
    operator_faces(2, residual, applied_ref)
    slope_source = applied_ref[...]
    for k in range(rows_y // per):
        piece = slope_source[:, k * LANES : (k + 1) * LANES]
        for j in range(per):
            press_ref[pl.ds(k * per + j, rows_x, stride=rows_y), :] = jnp.where(
                lane // depth == j, piece, 0.0
            )

    def differentiate(piece, index, carry):
        here = pl.ds(pl.multiple_of(index * chunk, chunk), chunk)
        part = strip(piece)
        source = split_dot(press_ref[here, :], spread_ref[:, part])
        pre_ref[here, part] = (source * slope_ref[here, part]).astype(BF16)
        return carry

    lax.fori_loop(0, steps, functools.partial(differentiate, 0), 0)
    give(1, 0, pre_ref, inv_ref)
    keep(0, pre_ref, inv_ref)
    lax.fori_loop(0, steps, functools.partial(differentiate, 1), 0)
    send(1, 0)
    give(1, 1, pre_ref, inv_ref)
    keep(1, pre_ref, inv_ref)
    send(1, 1)

    def mix_back(piece):
        g_real, g_imag = collect(1, piece)
        real = coef_ref[piece, 0]
        imaginary = coef_ref[piece, 1]
        in_real = jnp.zeros_like(real)
        in_imag = jnp.zeros_like(real)
        for shift in range(C):
            w_real, w_imag = weights(shift)
            back = (C - shift) % C
            in_real = in_real + group_roll(g_real * w_real + g_imag * w_imag, back)
            in_imag = in_imag + group_roll(g_imag * w_real - g_real * w_imag, back)
        mixed = jnp.concatenate([unlines(in_real), unlines(in_imag)], axis=0)
        gout_ref[piece, own] = mixed.astype(BF16)
        gather_push(gout_ref.at[piece], sem(1, piece, 2))
        for shift in range(C):
            c_real = group_roll(real, shift)
            c_imag = group_roll(imaginary, shift)
            both = (c_real * g_real + c_imag * g_imag, c_real * g_imag - c_imag * g_real)
            for which in range(2):
                total = both[which][:half]
                for k in range(1, parts):
                    total = total + both[which][k * half : (k + 1) * half]
                if piece > 0:
                    total = total + total_ref[which, shift]
                total_ref[which, shift] = total

    def weight_terms():
        spot = lane_iota((half, LANES))
        lines = []
        for which in range(2):
            grads = [jnp.zeros((half, LANES), F32) for _ in range(C * C // LANES)]
            for shift in range(C):
                total = total_ref[which, shift]
                turn = C
                while turn < LANES:
                    total = total + pltpu.roll(total, turn, 1)
                    turn *= 2
                for k in range(C * C // LANES):
                    source = k * (LANES // C) + spot // C
                    match = (spot % C - source + C) % C == shift
                    grads[k] = jnp.where(match, total, grads[k])
            lines.append(jnp.concatenate(grads, axis=1))
        terms_ref[own] = jnp.concatenate(lines, axis=0).astype(BF16)
        gather_push(terms_ref, sem(2, 0, 0))

    for piece in range(HALVES):
        if_owner(functools.partial(mix_back, piece))
    if_owner(weight_terms)

    def finish(piece, index, carry):
        here = pl.ds(pl.multiple_of(index * chunk, chunk), chunk)
        part = strip(piece)
        spectral = dot(fwd_ref[here, :], gout_ref[piece].reshape(columns, wide))
        total = spectral.astype(BF16).astype(F32) + dot(pre_ref[here, part], mix_t_ref[...])
        grad_ref[here, part] = total.astype(BF16)
        if piece == HALVES - 1:
            pltpu.make_async_copy(grad_ref.at[here], grad_out.at[here], store_sem).start()
        return carry

    staged(1, gout_ref, finish)
    gather_pass(terms_ref, sem(2, 0, 0))
    end_sends(1, gout_ref)
    gather_wait(terms_ref, sem(2, 0, 0))
    gather_end(terms_ref, sem(2, 0, 0))

    def report(k, carry):
        terms = terms_ref[k].astype(F32)
        spec_ref[0, k] = terms[:half]
        spec_ref[1, k] = terms[half:]
        return carry

    lax.fori_loop(0, owners, report, 0)
    pltpu.make_async_copy(grad_ref, grad_out, store_sem).wait()


def angle_tables(length, count, scale):
    frequencies = np.arange(count) - count // 2
    turns = np.arange(length)[:, None] * frequencies[None, :] % length
    angle = turns.astype(np.float32) * np.float32(2.0 * math.pi / length)
    return np.cos(angle) * np.float32(scale), np.sin(angle) * np.float32(scale)


def x_table(length):
    parts = []
    for scale in (1.0 / math.sqrt(length), 1.0 / math.sqrt(KX)):
        cosine, sine = angle_tables(length, KX, scale)
        parts += [cosine, -sine]
    table = np.concatenate(parts, axis=1)
    return np.pad(table, ((0, 0), (0, LANES - table.shape[1]))).astype(BF16)


def y_table(length):
    parts = []
    for scale in (1.0 / math.sqrt(length), 1.0 / math.sqrt(KY)):
        parts += list(angle_tables(length, KY, scale))
    table = np.concatenate(parts, axis=1)
    high = table.astype(BF16)
    low = (table - high.astype(np.float32)).astype(BF16)
    return np.concatenate([high, low], axis=1)


def shards(field, perm_class, perm_table, forcing, spec_weight, mix_weight, proj):
    gxn = lax.axis_size("gx")
    gyn = lax.axis_size("gy")
    n = gxn * gyn
    gx = lax.axis_index("gx")
    gy = lax.axis_index("gy")
    rows_x, rows_y, width = field.shape
    depth = width // C
    cells = rows_x * rows_y
    span_x = rows_x * gxn
    span_y = rows_y * gyn
    owners = min(n, KX * KY // 8)
    modes = KX * KY // owners
    block = 2 * modes
    columns = owners * block
    own = gx % 2 * (owners // 2) + (gx // 2 * gyn + gy) // (n // owners)
    weights = lax.dynamic_slice_in_dim(
        spec_weight.reshape(2, KX * KY, C, C), own * modes, modes, 1
    ).reshape(block, C * C)
    wide = width // HALVES
    step = wide

    vmem = pl.BlockSpec(memory_space=pltpu.VMEM)
    smem = pl.BlockSpec(memory_space=pltpu.SMEM)
    residual, grad_field, spec = pl.pallas_call(
        functools.partial(kernel, gxn, gyn, owners, rows_x, rows_y, depth),
        out_shape=(
            jax.ShapeDtypeStruct((rows_x, rows_y * depth), F32),
            jax.ShapeDtypeStruct((cells, width), BF16),
            jax.ShapeDtypeStruct((2, owners, modes, C * C), F32),
        ),
        in_specs=[pl.BlockSpec(memory_space=pl.ANY), vmem, smem] + [vmem] * 5 + [smem],
        out_specs=(vmem, pl.BlockSpec(memory_space=pl.ANY), vmem),
        scratch_shapes=[
            pltpu.VMEM((cells, width), BF16),
            pltpu.SemaphoreType.DMA,
            pltpu.VMEM((cells, width), BF16),
            pltpu.VMEM((cells, width), F32),
            pltpu.VMEM((rows_x, rows_y * depth), F32),
            pltpu.SemaphoreType.DMA,
            pltpu.VMEM((cells, columns), BF16),
            pltpu.VMEM((cells, columns), BF16),
            pltpu.VMEM((HALVES, owners, block, wide), BF16),
            pltpu.VMEM((2, HALVES, n // 2, block, wide), BF16),
            pltpu.VMEM((HALVES, owners, block, wide), BF16),
            pltpu.VMEM((HALVES, owners, block, wide), BF16),
            pltpu.VMEM((owners, block, C * C), BF16),
            pltpu.VMEM((2, C, modes, LANES), F32),
            pltpu.VMEM((cells, width), F32),
            pltpu.VMEM((cells, width), BF16),
            pltpu.VMEM((cells, LANES), F32),
            pltpu.VMEM((HALVES, 2, modes * wide // LANES, LANES), F32),
            pltpu.VMEM((2, HALVES, owners // 2, block, wide), BF16),
            pltpu.VMEM((HALVES, columns // 2, wide), F32),
            pltpu.VMEM((C, block, LANES), F32),
            pltpu.VMEM((step, step), BF16),
            pltpu.VMEM((step, step), BF16),
            pltpu.VMEM((1, width), F32),
            pltpu.VMEM((width, LANES), BF16),
            pltpu.VMEM((LANES, width), BF16),
            pltpu.VMEM((3, 2, 1, rows_y * depth), F32),
            pltpu.VMEM((3, 2, 1, rows_y * depth), F32),
            pltpu.VMEM((3, 2, rows_x, LANES), F32),
            pltpu.VMEM((3, 2, rows_x, LANES), F32),
            pltpu.SemaphoreType.DMA((18,)),
            pltpu.SemaphoreType.DMA((18,)),
            pltpu.SemaphoreType.DMA((3, 4)),
            pltpu.SemaphoreType.DMA((3, 4)),
        ],
        compiler_params=pltpu.CompilerParams(
            collective_id=0, has_side_effects=True, vmem_limit_bytes=60 * 1024 * 1024
        ),
        name="fourier_darcy",
    )(
        field.reshape(cells, width),
        perm_class,
        perm_table,
        forcing,
        jnp.asarray(x_table(span_x)),
        jnp.asarray(y_table(span_y)),
        weights,
        mix_weight,
        proj,
    )
    spec_grad = spec.reshape(2, KX, KY, C, C)
    return (residual, grad_field.reshape(rows_x, rows_y, width), spec_grad)


def solution(mesh):
    placed = (P("gx", "gy", None), P("gx", "gy"), P(), P("gx", "gy"), P(), P(), P())
    return jax.shard_map(
        shards,
        mesh=mesh,
        in_specs=placed,
        out_specs=(P("gx", "gy"), P("gx", "gy", None), P()),
        check_vma=False,
    )
```
